128 devices in a mesh: dp: 8 (over y, core), tensor: 16 (over z, x).
Axes of the slice: x: 4, y: 4, z: 4, core: 2. Of those that a mesh axis runs over, the one named last changes fastest.
Arguments:
- mixer_input: bfloat16 [512, 8192], P('dp', 'tensor'), may hold values from -6 to 6
- gate_input: bfloat16 [512, 8192], P('dp', 'tensor'), may hold values from -6 to 6
- conv_state: bfloat16 [512, 3, 8192], P('dp', None, 'tensor'), may hold values from -6 to 6
- conv_weight: float32 [4, 8192], P(None, 'tensor'), may hold values from -3 to 3
- conv_bias: float32 [8192], P('tensor'), may hold values from -0.5 to 0.5
- state_proj: bfloat16 [8192, 288], P('tensor'), may hold values from -0.0625 to 0.0625
- step_proj: bfloat16 [256, 8192], P(None, 'tensor'), may hold values from -0.375 to 0.375
- step_bias: float32 [8192], P('tensor'), may hold values from -3 to 0
- decay_rate: float32 [16, 8192], P(None, 'tensor'), may hold values from 0.5 to 16
- skip_gain: float32 [8192], P('tensor'), may hold values from 0.5 to 1.5
- scan_state: float32 [512, 16, 8192], P('dp', None, 'tensor'), may hold values from -6 to 6
- output_proj: bfloat16 [8192, 4096], P('tensor'), may hold values from -0.09375 to 0.09375
- residual: bfloat16 [512, 4096], P('dp', 'tensor'), may hold values from -6 to 6
- router: bfloat16 [4096, 8], replicated, may hold values from -0.09375 to 0.09375
- expert_ids: int32 [512, 2], P('dp'), may hold values from 0 to 7, all different within a row; in each aligned block of 64 rows (0 to 63, 64 to 127, ...) at most 40 rows name the same one
- active: int32 [512], P('dp'), may hold values 0 or 1
- up_weight: bfloat16 [8, 4096, 14336], P('dp', None, 'tensor'), may hold values from -0.09375 to 0.09375
- down_weight: bfloat16 [8, 14336, 4096], P('dp', 'tensor'), may hold values from -0.0625 to 0.0625
Outputs:
- layer_out: bfloat16 [512, 4096], P('dp', 'tensor')
- state_out: float32 [512, 16, 8192], P('dp', None, 'tensor')
- conv_cache: bfloat16 [512, 3, 8192], P('dp', None, 'tensor')
The draws below stay inside these ranges and needn't reach their ends.
Inputs may be any that keep to these rules, and one draw needn't show every extreme that they name: `expert_ids`: each row names two different experts; within each aligned block of 64 sessions (the sessions of one index of dp) no expert is named by more than 40 rows, a bound that some block reaches.
All inputs are finite; a program needn't handle non-finite values. No bound on the sum of `active` on one device may be relied on, other than what follows from the above.
Results may differ from the reference program's by a relative error of at most 0.02.
Values may be sent and summed in bfloat16 or wider, within the bound.
No kernel may reach another device: no remote copies, remote signals or barrier semaphores. Data moves between devices by JAX's collectives and lax.ppermute only.
A program may use at most 128 MiB of HBM per device.

```python
import math
import jax
import jax.numpy as jnp
import numpy as np
from jax import lax

DM = 4096
CH = 8192
NSTATE = 16
DT_RANK = 256
CONV = 4
FF = 14336
SESS_DEV = 64
SESSIONS = 512
CAP = 40
EXPERTS = 8
N_DP = 8
N_TENSOR = 16


def set_ends(drawn, rng, least, largest):
    extent = drawn.shape
    spot = [jax.random.randint(jax.random.fold_in(rng, axis), (), 0, extent[axis]) for axis in range(len(extent))]
    drawn = drawn.at[tuple(spot)].set(least)
    longest = extent.index(max(extent))
    spot[longest] = (spot[longest] + 1) % extent[longest]
    return drawn.at[tuple(spot)].set(largest)


def raised(array, stream_key, source, target, parts, factor):
    owner, partner = [(jnp.arange(array.shape[position]) // (array.shape[position] // parts)).reshape([-1 if axis == position else 1 for axis in range(array.ndim)]) for position in (source, target)]
    chosen = jax.random.permutation(stream_key, parts)[partner]
    strong = (owner == chosen) | (owner == (partner + parts // 2) % parts)
    return jnp.where(strong, factor * array, array)


def level_of(key, extent, cuts, low, largest):
    level, own = 1.0, jax.random.fold_in(key, 6)
    for axis_at, parts in cuts:
        heights = jnp.exp(jax.random.uniform(jax.random.fold_in(own, axis_at), (parts,), jnp.float32, low / len(cuts), largest / len(cuts)))
        level = level * jnp.repeat(heights, extent[axis_at] // parts).reshape([-1 if axis == axis_at else 1 for axis in range(len(extent))])
    return level


def shared_out(key, own, number, rows, count, top, limit, lean):
    sequence = jax.random.permutation(key, count)
    packed, usual = shares(count, rows * top, limit, lean, True), shares(count, rows * top, limit, lean, False)
    places = jnp.arange(count)

    def named(sizes, offset_by):
        used = int((sizes > 0).sum())
        fixed = max(1, used // 4)
        shifted = fixed + (places - fixed + offset_by * (used - fixed)) % max(1, count - fixed)
        return jnp.zeros((count,), jnp.int32).at[sequence[jnp.where(places < fixed, places, shifted)]].set(jnp.asarray(sizes, jnp.int32))

    sizes = jnp.where(number % 4 == 0, named(packed, number // 4), named(usual, number - number // 4 - 1))
    mixed = jax.random.permutation(jax.random.fold_in(own, 3), count)
    giver, receiver = mixed[0:count // 2 * 2:2], mixed[1:count // 2 * 2:2]
    room = jnp.minimum(sizes[giver] - 1, limit - sizes[receiver]) // 2
    room = jnp.where((giver == sequence[0]) | (receiver == sequence[0]) | (sizes[receiver] == 0), 0, jnp.maximum(room, 0))
    shifted = jax.random.randint(jax.random.fold_in(own, 4), (count // 2,), 0, 1 << 20) % (room + 1)
    sizes = sizes.at[giver].add(-shifted).at[receiver].add(shifted)
    members = jnp.searchsorted(jnp.cumsum(sizes), jnp.arange(rows * top), side="right").astype(jnp.int32)
    table = members.reshape(top, rows).T
    table = table[jax.random.permutation(jax.random.fold_in(own, 1), rows)]
    offset_by = jax.random.randint(jax.random.fold_in(own, 2), (rows, 1), 0, top)
    return jnp.take_along_axis(table, (jnp.arange(top)[None, :] + offset_by) % top, axis=1)


def shares(amount, total, reach, slope, full):
    portions = [(1 << 20) // math.isqrt(rank ** slope) + 1 for rank in range(1, amount + 1)]
    largest = reach if full else min(reach, max(-(-total // amount), total * portions[0] // sum(portions)))
    least = 1 if total - largest >= amount - 1 else 0
    counts, spare = [largest] + [least] * (amount - 1), total - largest - least * (amount - 1)
    while spare > 0:
        candidates = [i for i in range(1, amount) if counts[i] < largest] or [i for i in range(1, amount) if counts[i] < reach]
        mass, budget = sum([portions[i] for i in candidates]), spare
        for i in candidates:
            extra = min(reach - counts[i], max(1, budget * portions[i] // mass), spare)
            counts[i] = counts[i] + extra
            spare = spare - extra
    return np.array(counts)


def normal_values(stream_key, shape, scale, reach, cuts=(), kind=jnp.bfloat16):
    entries = scale * jax.random.normal(stream_key, shape, jnp.float32)
    if cuts:
        entries = entries * level_of(stream_key, shape, cuts, -0.22, 0.18)
    return jnp.clip(entries, -reach, reach).astype(kind)


def gaussian_with(stream_key, dims, scale, reach, cuts, heavy, kind=jnp.bfloat16):
    drawn = scale * jax.random.normal(stream_key, dims, jnp.float32)
    if cuts:
        drawn = drawn * level_of(stream_key, dims, cuts, -0.22, 0.18)
    return jnp.clip(raised(drawn, jax.random.fold_in(stream_key, 3), *heavy), -reach, reach).astype(kind)


def setup_inputs(seed: int = 0) -> dict:
    keys = jax.random.split(jax.random.key(seed), 19)
    mixer_input = normal_values(keys[0], (SESSIONS, CH), 1.0, 6.0, ((0, 8), (1, 16)))
    gate_input = normal_values(keys[1], (SESSIONS, CH), 1.0, 6.0, ((0, 8), (1, 16)))
    conv_state = normal_values(keys[2], (SESSIONS, CONV - 1, CH), 1.0, 6.0, ((0, 8), (2, 16)))
    conv_weight = normal_values(keys[3], (CONV, CH), CONV ** -0.5, 3.0, ((1, 16),), jnp.float32)
    conv_bias = jnp.clip(jax.random.uniform(keys[4], (CH,), jnp.float32, -0.5, 0.5) * level_of(keys[4], (CH,), ((0, 16),), -0.4, 0.0), -0.5, 0.5)
    state_proj = normal_values(keys[5], (CH, DT_RANK + 2 * NSTATE), CH ** -0.5, 0.0625, ((0, 16),))
    step_proj = normal_values(keys[6], (DT_RANK, CH), DT_RANK ** -0.5, 0.375, ((1, 16),))
    step_bias = jnp.clip(-3.0 + 3.0 * jax.random.uniform(keys[7], (CH,), jnp.float32) ** level_of(keys[7], (CH,), ((0, 16),), -0.2, 0.2), -3.0, 0.0)
    decay_rate = jnp.clip(jnp.exp(math.log(16.0) - 3.465736 * jax.random.uniform(keys[8], (NSTATE, CH), jnp.float32) ** level_of(keys[8], (NSTATE, CH), ((1, 16),), -0.2, 0.2)), 0.5, 16.0)
    skip_gain = jnp.clip(0.5 + 1.0 * jax.random.uniform(keys[9], (CH,), jnp.float32) ** level_of(keys[9], (CH,), ((0, 16),), -0.2, 0.2), 0.5, 1.5)
    scan_state = normal_values(keys[10], (SESSIONS, NSTATE, CH), 1.0, 6.0, ((0, 8), (2, 16)), jnp.float32)
    output_proj = gaussian_with(keys[11], (CH, DM), CH ** -0.5, 0.09375, ((0, 16),), (0, 1, 16, 2.0))
    residual = normal_values(keys[12], (SESSIONS, DM), 1.0, 6.0, ((0, 8), (1, 16)))
    router = normal_values(keys[13], (DM, EXPERTS), DM ** -0.5, 0.09375)
    expert_ids_keys = jax.random.split(jax.random.fold_in(keys[14], 1), SESSIONS // SESS_DEV)
    expert_ids_turns = jax.random.permutation(jax.random.fold_in(keys[14], 3), SESSIONS // SESS_DEV)
    expert_ids = jax.vmap(lambda own, number: shared_out(jax.random.fold_in(keys[14], 2), own, number, SESS_DEV, EXPERTS, 2, CAP, 2))(expert_ids_keys, expert_ids_turns).reshape((SESSIONS, 2))
    active = set_ends((jax.random.randint(keys[15], (SESSIONS,), 0, 4) < 3).astype(jnp.int32), jax.random.fold_in(keys[15], 1), 0, 1)
    up_weight = normal_values(keys[16], (EXPERTS, DM, FF), DM ** -0.5, 0.09375, ((0, 8), (2, 16)))
    down_weight = gaussian_with(keys[17], (EXPERTS, FF, DM), FF ** -0.5, 0.0625, ((0, 8), (1, 16)), (1, 2, 16, 2.0))
    return dict(mixer_input=mixer_input, gate_input=gate_input, conv_state=conv_state, conv_weight=conv_weight, conv_bias=conv_bias, state_proj=state_proj, step_proj=step_proj, step_bias=step_bias, decay_rate=decay_rate, skip_gain=skip_gain, scan_state=scan_state, output_proj=output_proj, residual=residual, router=router, expert_ids=expert_ids, active=active, up_weight=up_weight, down_weight=down_weight)


def reference(mixer_input, gate_input, conv_state, conv_weight, conv_bias, state_proj, step_proj, step_bias, decay_rate, skip_gain, scan_state, output_proj, residual, router, expert_ids, active, up_weight, down_weight):
    window = jnp.concatenate([conv_state, mixer_input[:, None, :]], axis=1)
    conv_sum = lax.optimization_barrier(jnp.sum(window.astype(jnp.float32) * conv_weight[None], axis=1)) + conv_bias
    conv_out = jax.nn.silu(conv_sum).astype(jnp.bfloat16)
    projected = jnp.dot(conv_out, state_proj, preferred_element_type=jnp.float32)
    step_raw = projected[:, :DT_RANK]
    input_map = projected[:, DT_RANK:DT_RANK + NSTATE]
    output_map = projected[:, DT_RANK + NSTATE:]
    step_norm = (step_raw * lax.rsqrt(lax.optimization_barrier(jnp.mean(step_raw * step_raw, axis=1, keepdims=True)) + 1e-06)).astype(jnp.bfloat16)
    step_size = jax.nn.softplus(jnp.dot(step_norm, step_proj, preferred_element_type=jnp.float32) + step_bias)
    conv_float = conv_out.astype(jnp.float32)
    state_next = jnp.exp(-step_size[:, None, :] * decay_rate[None]) * scan_state + (step_size * conv_float)[:, None, :] * input_map[:, :, None]
    live_float = active.astype(jnp.float32)
    live_mask = active == 1
    scan_out = lax.optimization_barrier(jnp.sum(output_map[:, :, None] * state_next, axis=1)) + skip_gain * conv_float
    gated = (scan_out * jax.nn.silu(gate_input.astype(jnp.float32)) * live_float[:, None]).astype(jnp.bfloat16)
    state_out = jnp.where(live_mask[:, None, None], state_next, scan_state)
    conv_cache = jnp.where(live_mask[:, None, None], window[:, 1:, :], conv_state)
    hidden_sum = residual.astype(jnp.float32) + jnp.dot(gated, output_proj, preferred_element_type=jnp.float32)
    inv_rms = lax.rsqrt(lax.optimization_barrier(jnp.sum(hidden_sum * hidden_sum, axis=1)) / DM + 1e-06)
    logits = jnp.dot(hidden_sum, router.astype(jnp.float32), precision=lax.Precision.HIGHEST) * inv_rms[:, None]
    normed = (hidden_sum * inv_rms[:, None]).astype(jnp.bfloat16)
    flat_ids = expert_ids.reshape(N_DP, SESS_DEV * 2)
    one_hot = (flat_ids[:, :, None] == jnp.arange(EXPERTS, dtype=jnp.int32)[None, None, :]).astype(jnp.int32)
    slot_index = lax.optimization_barrier(jnp.sum((jnp.cumsum(one_hot, axis=1) - one_hot) * one_hot, axis=2)).reshape(SESSIONS, 2)
    block_index = jnp.arange(SESSIONS, dtype=jnp.int32) // SESS_DEV
    target_row = block_index[:, None] * CAP + slot_index
    row_numbers = jnp.arange(N_DP * CAP, dtype=jnp.int32)
    block_width = FF // N_TENSOR

    def expert_rows(expert):
        picked = (expert_ids == expert) & live_mask[:, None]
        placement = lax.optimization_barrier(jnp.sum(((target_row[None] == row_numbers[:, None, None]) & picked[None]).astype(jnp.float32), axis=2)).astype(jnp.bfloat16)
        buffer = jnp.dot(placement, normed, preferred_element_type=jnp.float32).astype(jnp.bfloat16)
        hidden = jax.nn.silu(jnp.dot(buffer, up_weight[expert], preferred_element_type=jnp.float32)).astype(jnp.bfloat16)
        hidden_blocks = jnp.transpose(hidden.reshape(N_DP * CAP, N_TENSOR, block_width), (1, 0, 2))
        down_blocks = down_weight[expert].reshape(N_TENSOR, block_width, DM)

        def add_block(total, pieces):
            part = jnp.dot(pieces[0], pieces[1], preferred_element_type=jnp.float32).astype(jnp.bfloat16)
            return (total + part.astype(jnp.float32), None)
        total, unused = lax.scan(add_block, jnp.zeros((N_DP * CAP, DM), jnp.float32), (hidden_blocks, down_blocks))
        return total.astype(jnp.bfloat16)
    results = lax.map(expert_rows, jnp.arange(EXPERTS, dtype=jnp.int32))
    flat_results = results.reshape(EXPERTS * N_DP * CAP, DM)
    gathered = flat_results[expert_ids * (N_DP * CAP) + target_row]
    chosen_logit = jnp.take_along_axis(logits, expert_ids, axis=1)
    first = 1.0 / (1.0 + jnp.exp(chosen_logit[:, 1] - chosen_logit[:, 0]))
    second = 1.0 / (1.0 + jnp.exp(chosen_logit[:, 0] - chosen_logit[:, 1]))
    route_weight = jnp.stack([first, second], axis=1) * live_float[:, None]
    layer_out = (hidden_sum + lax.optimization_barrier(jnp.sum(route_weight[:, :, None] * gathered.astype(jnp.float32), axis=1))).astype(jnp.bfloat16)
    return (layer_out, state_out, conv_cache)
```

```python
import jax
import jax.numpy as jnp
from jax import lax
from jax.sharding import PartitionSpec as P

DM = 4096
CAP = 40
F32 = jnp.float32
BF16 = jnp.bfloat16


def sum_over_tensor(pieces):
    return jnp.sum(
        lax.all_to_all(pieces, "tensor", split_axis=0, concat_axis=0, tiled=True).astype(F32), axis=0
    )


def local(
    mixer_input,
    gate_input,
    conv_state,
    conv_weight,
    conv_bias,
    state_proj,
    step_proj,
    step_bias,
    decay_rate,
    skip_gain,
    scan_state,
    output_proj,
    residual,
    router,
    expert_ids,
    active,
    up_weight,
    down_weight,
):
    n_tensor = lax.axis_size("tensor")
    experts_total = router.shape[1]
    sessions = expert_ids.shape[0]
    slice_width = residual.shape[1]
    low_rank = step_proj.shape[0]
    states = decay_rate.shape[0]

    flat_ids = expert_ids.reshape(-1)
    pairs = jnp.arange(flat_ids.shape[0], dtype=jnp.int32)
    earlier = (flat_ids[:, None] == flat_ids[None, :]) & (pairs[None, :] < pairs[:, None])
    slot_index = jnp.sum(earlier.astype(jnp.int32), axis=1).reshape(sessions, 2)
    buffer_row = expert_ids * CAP + slot_index
    row_numbers = jnp.arange(experts_total * CAP, dtype=jnp.int32)
    live_float = active.astype(F32)
    live_mask = active == 1
    placement = jnp.any(
        (buffer_row[None] == row_numbers[:, None, None]) & live_mask[None, :, None], axis=2
    ).astype(BF16)

    window = jnp.concatenate([conv_state, mixer_input[:, None, :]], axis=1)
    conv_sum = jnp.sum(window.astype(F32) * conv_weight[None], axis=1) + conv_bias
    conv_out = jax.nn.silu(conv_sum).astype(BF16)
    partial_proj = jnp.dot(conv_out, state_proj, preferred_element_type=F32).astype(BF16)
    projected = sum_over_tensor(jnp.broadcast_to(partial_proj[None], (n_tensor,) + partial_proj.shape))
    step_raw = projected[:, :low_rank]
    input_map = projected[:, low_rank : low_rank + states]
    output_map = projected[:, low_rank + states :]
    step_norm = (
        step_raw * lax.rsqrt(jnp.mean(step_raw * step_raw, axis=1, keepdims=True) + 1e-06)
    ).astype(BF16)
    step_size = jax.nn.softplus(jnp.dot(step_norm, step_proj, preferred_element_type=F32) + step_bias)
    conv_float = conv_out.astype(F32)
    state_next = (
        jnp.exp(-step_size[:, None, :] * decay_rate[None]) * scan_state
        + (step_size * conv_float)[:, None, :] * input_map[:, :, None]
    )
    scan_out = jnp.sum(output_map[:, :, None] * state_next, axis=1) + skip_gain * conv_float
    gated = (scan_out * jax.nn.silu(gate_input.astype(F32)) * live_float[:, None]).astype(BF16)
    state_out = jnp.where(live_mask[:, None, None], state_next, scan_state)
    conv_cache = jnp.where(live_mask[:, None, None], window[:, 1:, :], conv_state)
    mixer_part = jnp.dot(gated, output_proj, preferred_element_type=F32).astype(BF16)
    hidden_local = sum_over_tensor(
        mixer_part.reshape(sessions, n_tensor, slice_width).transpose(1, 0, 2)
    ) + residual.astype(F32)

    outgoing = jnp.dot(placement, hidden_local.astype(BF16), preferred_element_type=F32).astype(BF16)
    incoming = lax.all_to_all(
        outgoing.reshape(experts_total, CAP, slice_width), "dp", split_axis=0, concat_axis=0, tiled=True
    ).reshape(experts_total * CAP, slice_width)
    columns = lax.all_to_all(
        jnp.broadcast_to(incoming[None], (n_tensor,) + incoming.shape),
        "tensor",
        split_axis=0,
        concat_axis=0,
        tiled=True,
    )
    rows = columns.transpose(1, 0, 2).reshape(experts_total * CAP, DM)
    rows_float = rows.astype(F32)
    inv_rms = lax.rsqrt(jnp.sum(rows_float * rows_float, axis=1) / DM + 1e-06)
    own_router = lax.dynamic_slice_in_dim(router, lax.axis_index("dp"), 1, 1)[:, 0].astype(F32)
    row_logit = jnp.sum(rows_float * own_router[None], axis=1) * inv_rms
    normed = (rows_float * inv_rms[:, None]).astype(BF16)
    up_sum = jnp.dot(normed, up_weight[0], preferred_element_type=F32)
    hidden = jax.nn.silu(up_sum).astype(BF16)
    expert_part = jnp.dot(hidden, down_weight[0], preferred_element_type=F32).astype(BF16)
    expert_share = sum_over_tensor(
        expert_part.reshape(experts_total * CAP, n_tensor, slice_width).transpose(1, 0, 2)
    ).astype(BF16)

    high = row_logit.astype(BF16)
    rest = row_logit - high.astype(F32)
    middle = rest.astype(BF16)
    low = (rest - middle.astype(F32)).astype(BF16)
    terms = jnp.stack([high, middle, low], axis=0).reshape(3, experts_total, CAP).transpose(1, 0, 2)
    terms = jnp.pad(terms, ((0, 0), (0, 5), (0, slice_width - CAP)))
    replies = jnp.concatenate([expert_share.reshape(experts_total, CAP, slice_width), terms], axis=1)
    returned = lax.all_to_all(replies, "dp", split_axis=0, concat_axis=0, tiled=True)
    returned_rows = returned[:, :CAP].reshape(experts_total * CAP, slice_width)
    returned_terms = returned[:, CAP : CAP + 3, :CAP].astype(F32)
    returned_logits = (
        returned_terms[:, 0] + (returned_terms[:, 1] + returned_terms[:, 2])
    ).reshape(-1)
    chosen = buffer_row.reshape(-1)[:, None] == row_numbers[None]
    gathered = jnp.dot(chosen.astype(BF16), returned_rows, preferred_element_type=F32).reshape(
        sessions, 2, slice_width
    )
    chosen_logit = jnp.sum(jnp.where(chosen, returned_logits[None], 0.0), axis=1).reshape(sessions, 2)
    first = 1.0 / (1.0 + jnp.exp(chosen_logit[:, 1] - chosen_logit[:, 0]))
    second = 1.0 / (1.0 + jnp.exp(chosen_logit[:, 0] - chosen_logit[:, 1]))
    route_weight = jnp.stack([first, second], axis=1) * live_float[:, None]
    layer_out = (hidden_local + jnp.sum(route_weight[:, :, None] * gathered, axis=1)).astype(BF16)
    return (layer_out, state_out, conv_cache)


def solution(mesh):
    placed = (
        P("dp", "tensor"),
        P("dp", "tensor"),
        P("dp", None, "tensor"),
        P(None, "tensor"),
        P("tensor"),
        P("tensor", None),
        P(None, "tensor"),
        P("tensor"),
        P(None, "tensor"),
        P("tensor"),
        P("dp", None, "tensor"),
        P("tensor", None),
        P("dp", "tensor"),
        P(),
        P("dp", None),
        P("dp"),
        P("dp", None, "tensor"),
        P("dp", "tensor", None),
    )
    return jax.shard_map(
        local,
        mesh=mesh,
        in_specs=placed,
        out_specs=(P("dp", "tensor"), P("dp", None, "tensor"), P("dp", None, "tensor")),
        check_vma=False,
    )
```

```python
import jax
import jax.numpy as jnp
from jax import lax
from jax.experimental import pallas as pl
from jax.experimental.pallas import tpu as pltpu
from jax.sharding import PartitionSpec as P

DM = 4096
CAP = 40
F32 = jnp.float32
BF16 = jnp.bfloat16
STEPS = 8
BUDGETS = (64, 96, 128, 160, 192, 224, 256, 320)


def sum_over_tensor(pieces):
    return jnp.sum(
        lax.all_to_all(pieces, "tensor", split_axis=0, concat_axis=0, tiled=True).astype(F32), axis=0
    )


def expert_kernel(
    cols_hbm, router_ref, up_hbm, down_hbm, part_hbm, terms_ref, cols, up, down, part, acc, sems
):
    tiles, rows, width = cols.shape
    pair = tiles // STEPS
    deep = pair * width

    def load_cols(c):
        return pltpu.make_async_copy(
            cols_hbm.at[pl.ds(c * pair, pair)], cols.at[pl.ds(c * pair, pair)], sems.at[0, c]
        )

    def load_up(c):
        return pltpu.make_async_copy(up_hbm.at[0, pl.ds(c * deep, deep)], up.at[c], sems.at[1, c])

    def load_down(c):
        return pltpu.make_async_copy(
            down_hbm.at[0, :, pl.ds(c * deep, deep)], down.at[c], sems.at[2, c]
        )

    def store_part(c):
        return pltpu.make_async_copy(
            part.at[pl.ds(c * pair, pair)], part_hbm.at[pl.ds(c * pair, pair)], sems.at[3, c]
        )

    for c in range(STEPS):
        load_cols(c).start()
        load_up(c).start()
    for c in range(STEPS):
        load_down(c).start()
    acc[...] = jnp.zeros_like(acc)

    def up_step(c, sums):
        squares, logits = sums
        load_cols(c).wait()
        load_up(c).wait()
        pieces = [cols[c * pair + i] for i in range(pair)]
        acc[...] += jnp.dot(
            jnp.concatenate(pieces, axis=1), up[c], preferred_element_type=F32
        )
        for i in range(pair):
            piece = pieces[i].astype(F32)
            squares = squares + jnp.sum(piece * piece, axis=1, keepdims=True)
            logits = logits + jnp.sum(
                piece * router_ref[pl.ds(c * pair + i, 1)], axis=1, keepdims=True
            )
        return squares, logits

    nothing = jnp.zeros((rows, 1), F32)
    squares, logits = lax.fori_loop(0, STEPS, up_step, (nothing, nothing))
    inv_rms = lax.rsqrt(squares / DM + 1e-06)
    up_sum = acc[...] * inv_rms
    hidden = (up_sum / (1.0 + jnp.exp(-up_sum))).astype(BF16)
    logit = logits * inv_rms
    high = logit.astype(BF16)
    rest = logit - high.astype(F32)
    middle = rest.astype(BF16)
    low = rest - middle.astype(F32)
    lane = lax.broadcasted_iota(jnp.int32, (rows, 128), 1)
    terms_ref[...] = jnp.where(
        lane == 0,
        high.astype(F32),
        jnp.where(lane == 1, middle.astype(F32), jnp.where(lane == 2, low, 0.0)),
    ).astype(BF16)

    def down_step(c, carry):
        load_down(c).wait()
        out = jnp.dot(hidden, down[c], preferred_element_type=F32).astype(BF16)
        for i in range(pair):
            part[c * pair + i] = out[:, i * width : (i + 1) * width]
        store_part(c).start()
        return carry

    lax.fori_loop(0, STEPS, down_step, 0)
    for c in range(STEPS):
        store_part(c).wait()


def expert(columns, own_router, up_weight, down_weight):
    tiles, rows, width = columns.shape
    hidden_units = up_weight.shape[2]
    deep = tiles // STEPS * width
    anywhere = pl.BlockSpec(memory_space=pl.ANY)
    vmem = pl.BlockSpec(memory_space=pltpu.VMEM)
    return pl.pallas_call(
        expert_kernel,
        out_shape=(
            jax.ShapeDtypeStruct((tiles, rows, width), BF16),
            jax.ShapeDtypeStruct((rows, 128), BF16),
        ),
        in_specs=[anywhere, vmem, anywhere, anywhere],
        out_specs=(anywhere, vmem),
        scratch_shapes=[
            pltpu.VMEM((tiles, rows, width), BF16),
            pltpu.VMEM((STEPS, deep, hidden_units), BF16),
            pltpu.VMEM((STEPS, hidden_units, deep), BF16),
            pltpu.VMEM((tiles, rows, width), BF16),
            pltpu.VMEM((rows, hidden_units), F32),
            pltpu.SemaphoreType.DMA((4, STEPS)),
        ],
        compiler_params=pltpu.CompilerParams(vmem_limit_bytes=40 * 2**20),
        cost_estimate=pl.CostEstimate(
            flops=4 * rows * tiles * width * hidden_units,
            bytes_accessed=4 * tiles * width * (hidden_units + rows),
            transcendentals=rows * hidden_units,
        ),
        name="expert",
    )(columns, own_router, up_weight, down_weight)


def local(
    mixer_input,
    gate_input,
    conv_state,
    conv_weight,
    conv_bias,
    state_proj,
    step_proj,
    step_bias,
    decay_rate,
    skip_gain,
    scan_state,
    output_proj,
    residual,
    router,
    expert_ids,
    active,
    up_weight,
    down_weight,
):
    n_tensor = lax.axis_size("tensor")
    experts_total = router.shape[1]
    sessions = expert_ids.shape[0]
    slice_width = residual.shape[1]
    low_rank = step_proj.shape[0]
    states = decay_rate.shape[0]

    live_float = active.astype(F32)
    live_mask = active == 1
    flat_ids = expert_ids.reshape(-1)
    flat_live = jnp.broadcast_to(live_mask[:, None], (sessions, 2)).reshape(-1)
    pairs = jnp.arange(flat_ids.shape[0], dtype=jnp.int32)
    earlier = (
        (flat_ids[:, None] == flat_ids[None, :])
        & (pairs[None, :] < pairs[:, None])
        & flat_live[None, :]
    )
    slot_index = jnp.sum(earlier.astype(jnp.int32), axis=1).reshape(sessions, 2)
    buffer_row = jnp.where(live_mask[:, None], expert_ids * CAP + slot_index, -1)
    row_numbers = jnp.arange(experts_total * CAP, dtype=jnp.int32)
    placement = jnp.any(buffer_row[None] == row_numbers[:, None, None], axis=2).astype(BF16)
    live_counts = jnp.sum(
        (flat_ids[None] == jnp.arange(experts_total, dtype=jnp.int32)[:, None]) & flat_live[None],
        axis=1,
    ).astype(BF16)

    window = jnp.concatenate([conv_state, mixer_input[:, None, :]], axis=1)
    conv_sum = jnp.sum(window.astype(F32) * conv_weight[None], axis=1) + conv_bias
    conv_out = jax.nn.silu(conv_sum).astype(BF16)
    partial_proj = jnp.dot(conv_out, state_proj, preferred_element_type=F32).astype(BF16)
    projected = sum_over_tensor(jnp.broadcast_to(partial_proj[None], (n_tensor,) + partial_proj.shape))
    step_raw = projected[:, :low_rank]
    input_map = projected[:, low_rank : low_rank + states]
    output_map = projected[:, low_rank + states :]
    step_norm = (
        step_raw * lax.rsqrt(jnp.mean(step_raw * step_raw, axis=1, keepdims=True) + 1e-06)
    ).astype(BF16)
    step_size = jax.nn.softplus(jnp.dot(step_norm, step_proj, preferred_element_type=F32) + step_bias)
    conv_float = conv_out.astype(F32)
    state_next = (
        jnp.exp(-step_size[:, None, :] * decay_rate[None]) * scan_state
        + (step_size * conv_float)[:, None, :] * input_map[:, :, None]
    )
    scan_out = jnp.sum(output_map[:, :, None] * state_next, axis=1) + skip_gain * conv_float
    gated = (scan_out * jax.nn.silu(gate_input.astype(F32)) * live_float[:, None]).astype(BF16)
    state_out = jnp.where(live_mask[:, None, None], state_next, scan_state)
    conv_cache = jnp.where(live_mask[:, None, None], window[:, 1:, :], conv_state)
    mixer_part = jnp.dot(gated, output_proj, preferred_element_type=F32).astype(BF16)
    hidden_local = sum_over_tensor(
        mixer_part.reshape(sessions, n_tensor, slice_width).transpose(1, 0, 2)
    ) + residual.astype(F32)

    outgoing = jnp.dot(placement, hidden_local.astype(BF16), preferred_element_type=F32).astype(BF16)
    outgoing = jnp.concatenate(
        [
            outgoing.reshape(experts_total, CAP, slice_width),
            jnp.broadcast_to(live_counts[:, None, None], (experts_total, 8, slice_width)),
        ],
        axis=1,
    )
    incoming = lax.all_to_all(outgoing, "dp", split_axis=0, concat_axis=0, tiled=True)
    counts = incoming[:, CAP, 0].astype(F32).astype(jnp.int32)
    blocks = counts.shape[0]
    before = jnp.arange(blocks)[None, :] < jnp.arange(blocks)[:, None]
    first_row = jnp.sum(jnp.where(before, counts[None], 0), axis=1)
    slots = jnp.arange(CAP, dtype=jnp.int32)[None]
    packed_row = jnp.where(slots < counts[:, None], first_row[:, None] + slots, -1).reshape(-1)
    packing = (packed_row[None] == row_numbers[:, None]).astype(BF16)
    packed = jnp.dot(
        packing, incoming[:, :CAP].reshape(-1, slice_width), preferred_element_type=F32
    ).astype(BF16)
    own_router = lax.dynamic_slice_in_dim(router, lax.axis_index("dp"), 1, 1)[:, 0]
    own_router = own_router.astype(F32).reshape(n_tensor, slice_width)

    def on_rows(rows):
        def run(packed, packing, own_router, up_weight, down_weight):
            columns = lax.all_to_all(
                jnp.broadcast_to(packed[None, :rows], (n_tensor, rows, slice_width)),
                "tensor",
                split_axis=0,
                concat_axis=0,
                tiled=True,
            )
            expert_part, terms = expert(columns, own_router, up_weight, down_weight)
            share = jnp.concatenate([sum_over_tensor(expert_part).astype(BF16), terms], axis=1)
            return lax.dot_general(
                packing[:rows], share, (((0,), (0,)), ((), ())), preferred_element_type=F32
            ).astype(BF16)

        return run

    needed = jnp.sum(counts)
    budget = jnp.sum((needed > jnp.asarray(BUDGETS[:-1], jnp.int32)).astype(jnp.int32))
    replies = lax.switch(
        budget, [on_rows(rows) for rows in BUDGETS], packed, packing, own_router, up_weight, down_weight
    )

    returned = lax.all_to_all(
        replies.reshape(experts_total, CAP, slice_width + 128),
        "dp",
        split_axis=0,
        concat_axis=0,
        tiled=True,
    ).reshape(experts_total * CAP, slice_width + 128)
    chosen = buffer_row.reshape(-1)[:, None] == row_numbers[None]
    gathered = jnp.dot(chosen.astype(BF16), returned, preferred_element_type=F32).reshape(
        sessions, 2, slice_width + 128
    )
    chosen_logit = gathered[:, :, slice_width] + (
        gathered[:, :, slice_width + 1] + gathered[:, :, slice_width + 2]
    )
    first = 1.0 / (1.0 + jnp.exp(chosen_logit[:, 1] - chosen_logit[:, 0]))
    second = 1.0 / (1.0 + jnp.exp(chosen_logit[:, 0] - chosen_logit[:, 1]))
    route_weight = jnp.stack([first, second], axis=1) * live_float[:, None]
    layer_out = (hidden_local + jnp.sum(route_weight[:, :, None] * gathered[:, :, :slice_width], axis=1)).astype(BF16)
    return (layer_out, state_out, conv_cache)


def solution(mesh):
    placed = (
        P("dp", "tensor"),
        P("dp", "tensor"),
        P("dp", None, "tensor"),
        P(None, "tensor"),
        P("tensor"),
        P("tensor", None),
        P(None, "tensor"),
        P("tensor"),
        P(None, "tensor"),
        P("tensor"),
        P("dp", None, "tensor"),
        P("tensor", None),
        P("dp", "tensor"),
        P(),
        P("dp", None),
        P("dp"),
        P("dp", None, "tensor"),
        P("dp", "tensor", None),
    )
    return jax.shard_map(
        local,
        mesh=mesh,
        in_specs=placed,
        out_specs=(P("dp", "tensor"), P("dp", None, "tensor"), P("dp", None, "tensor")),
        check_vma=False,
    )
```

```python
import math

import jax
import jax.numpy as jnp
from jax import lax
from jax.experimental import pallas as pl
from jax.experimental.pallas import tpu as pltpu
from jax.sharding import PartitionSpec as P

DM = 4096
CAP = 40
F32 = jnp.float32
BF16 = jnp.bfloat16
STEPS = 8
BUDGETS = (64, 80, 96, 112, 128, 144, 160, 176, 192, 208, 224, 240, 256, 288, 320)
GROUP = 8


def sum_over_tensor(pieces):
    return jnp.sum(
        lax.all_to_all(pieces, "tensor", split_axis=0, concat_axis=0, tiled=True).astype(F32), axis=0
    )


def sum_everywhere(piece):
    count = lax.axis_size("tensor")
    side = math.isqrt(count)
    for along_z in (True, False):
        total = piece.astype(F32)
        for step in range(1, side):
            ring = []
            for i in range(count):
                z, x = i // side, i % side
                if along_z:
                    z = (z + step) % side
                else:
                    x = (x + step) % side
                ring.append((i, z * side + x))
            total = total + lax.ppermute(piece, "tensor", ring).astype(F32)
        piece = total.astype(BF16)
    return total


def state_kernel(
    live_scalar,
    projected_ref,
    conv_ref,
    gate_ref,
    live_ref,
    step_proj_ref,
    step_bias_ref,
    decay_ref,
    skip_ref,
    scan_hbm,
    proj_hbm,
    state_hbm,
    part_ref,
    state,
    proj,
    step,
    drive,
    mixed,
    sems,
):
    sessions, states, channels = state.shape
    groups = sessions // GROUP
    tiles, depth, width = proj.shape
    low_rank = step_proj_ref.shape[0]

    def load_scan(g):
        part = pl.ds(g * GROUP, GROUP)
        return pltpu.make_async_copy(scan_hbm.at[part], state.at[part], sems.at[0, g])

    def load_proj(j):
        return pltpu.make_async_copy(
            proj_hbm.at[:, pl.ds(j * width, width)], proj.at[j], sems.at[1, j]
        )

    def store_state(g):
        part = pl.ds(g * GROUP, GROUP)
        return pltpu.make_async_copy(state.at[part], state_hbm.at[part], sems.at[2, g])

    for g in range(groups):
        load_scan(g).start()
    for j in range(tiles):
        load_proj(j).start()
    projected = projected_ref[...]
    step_raw = projected[:, :low_rank]
    step_norm = (
        step_raw * lax.rsqrt(jnp.mean(step_raw * step_raw, axis=1, keepdims=True) + 1e-06)
    ).astype(BF16)
    before = jnp.dot(step_norm, step_proj_ref[...], preferred_element_type=F32) + step_bias_ref[...]
    step_size = jnp.maximum(before, 0.0) + jnp.log1p(jnp.exp(-jnp.abs(before)))
    conv_float = conv_ref[...].astype(F32)
    step[...] = step_size
    drive[...] = step_size * conv_float
    maps = projected[:, low_rank : low_rank + 2 * states]
    maps = jnp.concatenate([maps, jnp.zeros((sessions, 128 - 2 * states), F32)], axis=1).T
    decay = decay_ref[...]
    for g in range(groups):
        load_scan(g).wait()
        for s in range(g * GROUP, (g + 1) * GROUP):
            old = state[s]
            new = (
                jnp.exp(-step[s : s + 1] * decay) * old + drive[s : s + 1] * maps[:states, s : s + 1]
            )
            mixed[s : s + 1] = jnp.sum(new * maps[states : 2 * states, s : s + 1], axis=0, keepdims=True)
            state[s] = jnp.where(live_scalar[s] == 1, new, old)
        store_state(g).start()
    gate = gate_ref[...].astype(F32)
    scan_out = mixed[...] + skip_ref[...] * conv_float
    gated = (scan_out * (gate / (1.0 + jnp.exp(-gate))) * live_ref[...]).astype(BF16)
    for j in range(tiles):
        load_proj(j).wait()
        part_ref[j] = jnp.dot(gated, proj[j], preferred_element_type=F32).astype(BF16)
    for g in range(groups):
        store_state(g).wait()


def state_step(
    active, projected, conv_out, gate_input, step_proj, step_bias, decay_rate, skip_gain, scan_state, output_proj, tiles
):
    sessions, states, channels = scan_state.shape
    width = output_proj.shape[1] // tiles
    anywhere = pl.BlockSpec(memory_space=pl.ANY)
    vmem = pl.BlockSpec(memory_space=pltpu.VMEM)
    smem = pl.BlockSpec(memory_space=pltpu.SMEM)
    return pl.pallas_call(
        state_kernel,
        out_shape=(
            jax.ShapeDtypeStruct(scan_state.shape, F32),
            jax.ShapeDtypeStruct((tiles, sessions, width), BF16),
        ),
        in_specs=[smem] + [vmem] * 8 + [anywhere] * 2,
        out_specs=(anywhere, vmem),
        scratch_shapes=[
            pltpu.VMEM(scan_state.shape, F32),
            pltpu.VMEM((tiles, channels, width), BF16),
            pltpu.VMEM((sessions, channels), F32),
            pltpu.VMEM((sessions, channels), F32),
            pltpu.VMEM((sessions, channels), F32),
            pltpu.SemaphoreType.DMA((3, max(tiles, sessions // GROUP))),
        ],
        compiler_params=pltpu.CompilerParams(vmem_limit_bytes=24 * 2**20),
        cost_estimate=pl.CostEstimate(
            flops=2 * sessions * channels * (tiles * width + 512),
            bytes_accessed=8 * scan_state.size + 2 * output_proj.size,
            transcendentals=scan_state.size,
        ),
        name="state",
    )(
        active,
        projected,
        conv_out,
        gate_input,
        active.astype(F32)[:, None],
        step_proj,
        step_bias[None],
        decay_rate,
        skip_gain[None],
        scan_state,
        output_proj,
    )


def packing_kernel(incoming_ref, packed_ref, spread_ref, needed_ref):
    blocks, block_rows, width = incoming_ref.shape
    packed_rows = packed_ref.shape[0]
    counts = [incoming_ref[b].astype(F32)[CAP:, :128] for b in range(blocks)]
    lanes = blocks * block_rows
    lane = lax.broadcasted_iota(jnp.int32, (8, lanes), 1).astype(F32)
    slot = lax.broadcasted_iota(jnp.int32, (CAP, 128), 0).astype(F32)
    target = jnp.full((8, lanes), -1.0, F32)
    first = jnp.zeros((8, 128), F32)
    columns = []
    for b in range(blocks):
        wide_count = jnp.concatenate([counts[b]] * (lanes // 128), axis=1)
        wide_first = jnp.concatenate([first] * (lanes // 128), axis=1)
        place = lane - b * block_rows
        target = jnp.where((place >= 0) & (place < wide_count), wide_first + place, target)
        columns.append(jnp.where(slot < counts[b][0:1], first[0:1] + slot, -1.0))
        first = first + counts[b]
    row = lax.broadcasted_iota(jnp.int32, (packed_rows, lanes), 0).astype(F32)
    packing = jnp.where(row == target[0:1], 1.0, 0.0).astype(BF16)
    incoming = jnp.concatenate([incoming_ref[b] for b in range(blocks)], axis=0)
    packed_ref[...] = jnp.dot(packing, incoming, preferred_element_type=F32).astype(BF16)
    column = jnp.concatenate(columns, axis=0)
    wide = spread_ref.shape[1]
    lane = lax.broadcasted_iota(jnp.int32, (blocks * CAP, wide), 1).astype(F32)
    column = jnp.concatenate([column] * (wide // 128), axis=1)
    spread_ref[...] = jnp.where(lane == column, 1.0, 0.0).astype(BF16)
    needed_ref[0] = jnp.max(first).astype(jnp.int32)


def pack(incoming):
    blocks, block_rows, width = incoming.shape
    rows = blocks * CAP
    vmem = pl.BlockSpec(memory_space=pltpu.VMEM)
    return pl.pallas_call(
        packing_kernel,
        out_shape=(
            jax.ShapeDtypeStruct((rows, width), BF16),
            jax.ShapeDtypeStruct((rows, blocks * block_rows), BF16),
            jax.ShapeDtypeStruct((1,), jnp.int32),
        ),
        in_specs=[vmem],
        out_specs=(vmem, vmem, pl.BlockSpec(memory_space=pltpu.SMEM)),
        name="pack",
    )(incoming)


def expert_kernel(
    cols_hbm, router_ref, up_hbm, down_hbm, part_hbm, terms_ref, cols, up, down, part, acc, sems
):
    tiles, rows, width = cols.shape
    pair = tiles // STEPS
    deep = pair * width

    def load_cols(c):
        return pltpu.make_async_copy(
            cols_hbm.at[pl.ds(c * pair, pair)], cols.at[pl.ds(c * pair, pair)], sems.at[0, c]
        )

    def load_up(c):
        return pltpu.make_async_copy(up_hbm.at[0, pl.ds(c * deep, deep)], up.at[c], sems.at[1, c])

    def load_down(c):
        return pltpu.make_async_copy(
            down_hbm.at[0, :, pl.ds(c * deep, deep)], down.at[c], sems.at[2, c]
        )

    def store_part(c):
        return pltpu.make_async_copy(
            part.at[pl.ds(c * pair, pair)], part_hbm.at[pl.ds(c * pair, pair)], sems.at[3, c]
        )

    for c in range(STEPS):
        load_cols(c).start()
        load_up(c).start()
    for c in range(STEPS):
        load_down(c).start()
    acc[...] = jnp.zeros_like(acc)

    def up_step(c, sums):
        squares, logits = sums
        load_cols(c).wait()
        load_up(c).wait()
        pieces = [cols[c * pair + i] for i in range(pair)]
        acc[...] += jnp.dot(
            jnp.concatenate(pieces, axis=1), up[c], preferred_element_type=F32
        )
        for i in range(pair):
            piece = pieces[i].astype(F32)
            squares = squares + jnp.sum(piece * piece, axis=1, keepdims=True)
            logits = logits + jnp.sum(
                piece * router_ref[pl.ds(c * pair + i, 1)], axis=1, keepdims=True
            )
        return squares, logits

    nothing = jnp.zeros((rows, 1), F32)
    squares, logits = lax.fori_loop(0, STEPS, up_step, (nothing, nothing))
    inv_rms = lax.rsqrt(squares / DM + 1e-06)
    up_sum = acc[...] * inv_rms
    hidden = (up_sum / (1.0 + jnp.exp(-up_sum))).astype(BF16)
    logit = logits * inv_rms
    high = logit.astype(BF16)
    rest = logit - high.astype(F32)
    middle = rest.astype(BF16)
    low = rest - middle.astype(F32)
    lane = lax.broadcasted_iota(jnp.int32, (rows, 128), 1)
    terms_ref[...] = jnp.where(
        lane == 0,
        high.astype(F32),
        jnp.where(lane == 1, middle.astype(F32), jnp.where(lane == 2, low, 0.0)),
    ).astype(BF16)

    def down_step(c, carry):
        load_down(c).wait()
        out = jnp.dot(hidden, down[c], preferred_element_type=F32).astype(BF16)
        for i in range(pair):
            part[c * pair + i] = out[:, i * width : (i + 1) * width]
        store_part(c).start()
        return carry

    lax.fori_loop(0, STEPS, down_step, 0)
    for c in range(STEPS):
        store_part(c).wait()


def expert(columns, own_router, up_weight, down_weight):
    tiles, rows, width = columns.shape
    hidden_units = up_weight.shape[2]
    deep = tiles // STEPS * width
    anywhere = pl.BlockSpec(memory_space=pl.ANY)
    vmem = pl.BlockSpec(memory_space=pltpu.VMEM)
    return pl.pallas_call(
        expert_kernel,
        out_shape=(
            jax.ShapeDtypeStruct((tiles, rows, width), BF16),
            jax.ShapeDtypeStruct((rows, 128), BF16),
        ),
        in_specs=[anywhere, vmem, anywhere, anywhere],
        out_specs=(anywhere, vmem),
        scratch_shapes=[
            pltpu.VMEM((tiles, rows, width), BF16),
            pltpu.VMEM((STEPS, deep, hidden_units), BF16),
            pltpu.VMEM((STEPS, hidden_units, deep), BF16),
            pltpu.VMEM((tiles, rows, width), BF16),
            pltpu.VMEM((rows, hidden_units), F32),
            pltpu.SemaphoreType.DMA((4, STEPS)),
        ],
        compiler_params=pltpu.CompilerParams(vmem_limit_bytes=40 * 2**20),
        cost_estimate=pl.CostEstimate(
            flops=4 * rows * tiles * width * hidden_units,
            bytes_accessed=4 * tiles * width * (hidden_units + rows),
            transcendentals=rows * hidden_units,
        ),
        name="expert",
    )(columns, own_router, up_weight, down_weight)


def local(
    mixer_input,
    gate_input,
    conv_state,
    conv_weight,
    conv_bias,
    state_proj,
    step_proj,
    step_bias,
    decay_rate,
    skip_gain,
    scan_state,
    output_proj,
    residual,
    router,
    expert_ids,
    active,
    up_weight,
    down_weight,
):
    n_tensor = lax.axis_size("tensor")
    experts_total = router.shape[1]
    sessions = expert_ids.shape[0]
    slice_width = residual.shape[1]

    live_float = active.astype(F32)
    live_mask = active == 1
    flat_ids = expert_ids.reshape(-1)
    flat_live = jnp.broadcast_to(live_mask[:, None], (sessions, 2)).reshape(-1)
    pairs = jnp.arange(flat_ids.shape[0], dtype=jnp.int32)
    earlier = (
        (flat_ids[:, None] == flat_ids[None, :])
        & (pairs[None, :] < pairs[:, None])
        & flat_live[None, :]
    )
    slot_index = jnp.sum(earlier.astype(jnp.int32), axis=1).reshape(sessions, 2)
    buffer_row = jnp.where(live_mask[:, None], expert_ids * CAP + slot_index, -1)
    row_numbers = jnp.arange(experts_total * CAP, dtype=jnp.int32)
    placement = jnp.any(buffer_row[None] == row_numbers[:, None, None], axis=2).astype(BF16)
    live_counts = jnp.sum(
        (flat_ids[None] == jnp.arange(experts_total, dtype=jnp.int32)[:, None]) & flat_live[None],
        axis=1,
    ).astype(BF16)

    window = jnp.concatenate([conv_state, mixer_input[:, None, :]], axis=1)
    conv_sum = jnp.sum(window.astype(F32) * conv_weight[None], axis=1) + conv_bias
    conv_out = jax.nn.silu(conv_sum).astype(BF16)
    partial_proj = jnp.dot(conv_out, state_proj, preferred_element_type=F32).astype(BF16)
    projected = sum_everywhere(partial_proj)
    state_out, mixer_part = state_step(
        active,
        projected,
        conv_out,
        gate_input,
        step_proj,
        step_bias,
        decay_rate,
        skip_gain,
        scan_state,
        output_proj,
        n_tensor,
    )
    conv_cache = jnp.where(live_mask[:, None, None], window[:, 1:, :], conv_state)
    hidden_local = sum_over_tensor(mixer_part) + residual.astype(F32)

    outgoing = jnp.dot(placement, hidden_local.astype(BF16), preferred_element_type=F32).astype(BF16)
    outgoing = jnp.concatenate(
        [
            outgoing.reshape(experts_total, CAP, slice_width),
            jnp.broadcast_to(live_counts[:, None, None], (experts_total, 8, slice_width)),
        ],
        axis=1,
    )
    incoming = lax.all_to_all(outgoing, "dp", split_axis=0, concat_axis=0, tiled=True)
    packed, spread, needed = pack(incoming)
    own_router = lax.dynamic_slice_in_dim(router, lax.axis_index("dp"), 1, 1)[:, 0]
    own_router = own_router.astype(F32).reshape(n_tensor, slice_width)

    def on_rows(rows):
        def run(packed, spread, own_router, up_weight, down_weight):
            columns = lax.all_to_all(
                jnp.broadcast_to(packed[None, :rows], (n_tensor, rows, slice_width)),
                "tensor",
                split_axis=0,
                concat_axis=0,
                tiled=True,
            )
            expert_part, terms = expert(columns, own_router, up_weight, down_weight)
            share = jnp.concatenate([sum_over_tensor(expert_part).astype(BF16), terms], axis=1)
            return jnp.dot(spread[:, :rows], share, preferred_element_type=F32).astype(BF16)

        return run

    budget = jnp.sum((needed[0] > jnp.asarray(BUDGETS[:-1], jnp.int32)).astype(jnp.int32))
    replies = lax.switch(
        budget, [on_rows(rows) for rows in BUDGETS], packed, spread, own_router, up_weight, down_weight
    )

    returned = lax.all_to_all(
        replies.reshape(experts_total, CAP, slice_width + 128),
        "dp",
        split_axis=0,
        concat_axis=0,
        tiled=True,
    ).reshape(experts_total * CAP, slice_width + 128)
    chosen = buffer_row.reshape(-1)[:, None] == row_numbers[None]
    gathered = jnp.dot(chosen.astype(BF16), returned, preferred_element_type=F32).reshape(
        sessions, 2, slice_width + 128
    )
    chosen_logit = gathered[:, :, slice_width] + (
        gathered[:, :, slice_width + 1] + gathered[:, :, slice_width + 2]
    )
    first = 1.0 / (1.0 + jnp.exp(chosen_logit[:, 1] - chosen_logit[:, 0]))
    second = 1.0 / (1.0 + jnp.exp(chosen_logit[:, 0] - chosen_logit[:, 1]))
    route_weight = jnp.stack([first, second], axis=1) * live_float[:, None]
    layer_out = (hidden_local + jnp.sum(route_weight[:, :, None] * gathered[:, :, :slice_width], axis=1)).astype(BF16)
    return (layer_out, state_out, conv_cache)


def solution(mesh):
    placed = (
        P("dp", "tensor"),
        P("dp", "tensor"),
        P("dp", None, "tensor"),
        P(None, "tensor"),
        P("tensor"),
        P("tensor", None),
        P(None, "tensor"),
        P("tensor"),
        P(None, "tensor"),
        P("tensor"),
        P("dp", None, "tensor"),
        P("tensor", None),
        P("dp", "tensor"),
        P(),
        P("dp", None),
        P("dp"),
        P("dp", None, "tensor"),
        P("dp", "tensor", None),
    )
    return jax.shard_map(
        local,
        mesh=mesh,
        in_specs=placed,
        out_specs=(P("dp", "tensor"), P("dp", None, "tensor"), P("dp", None, "tensor")),
        check_vma=False,
    )
```

```python
import math

import jax
import jax.numpy as jnp
from jax import lax
from jax.experimental import pallas as pl
from jax.experimental.pallas import tpu as pltpu
from jax.sharding import PartitionSpec as P

DM = 4096
CAP = 40
F32 = jnp.float32
BF16 = jnp.bfloat16
STEPS = 8
BUDGETS = (64, 96, 128, 160, 192, 240, 256, 320)


def sum_over_tensor(pieces):
    return jnp.sum(
        lax.all_to_all(pieces, "tensor", split_axis=0, concat_axis=0, tiled=True).astype(F32), axis=0
    )


def sum_everywhere(piece):
    count = lax.axis_size("tensor")
    side = math.isqrt(count)
    for along_z in (True, False):
        total = piece.astype(F32)
        for step in range(1, side):
            ring = []
            for i in range(count):
                z, x = i // side, i % side
                if along_z:
                    z = (z + step) % side
                else:
                    x = (x + step) % side
                ring.append((i, z * side + x))
            total = total + lax.ppermute(piece, "tensor", ring).astype(F32)
        piece = total.astype(BF16)
    return total


def packing_kernel(incoming_ref, packed_ref, spread_ref, budget_ref):
    blocks, block_rows, width = incoming_ref.shape
    packed_rows = packed_ref.shape[0]
    counts = [incoming_ref[b].astype(F32)[CAP:, :128] for b in range(blocks)]
    lanes = blocks * block_rows
    lane = lax.broadcasted_iota(jnp.int32, (8, lanes), 1).astype(F32)
    slot = lax.broadcasted_iota(jnp.int32, (CAP, 128), 0).astype(F32)
    target = jnp.full((8, lanes), -1.0, F32)
    first = jnp.zeros((8, 128), F32)
    columns = []
    for b in range(blocks):
        wide_count = jnp.concatenate([counts[b]] * (lanes // 128), axis=1)
        wide_first = jnp.concatenate([first] * (lanes // 128), axis=1)
        place = lane - b * block_rows
        target = jnp.where((place >= 0) & (place < wide_count), wide_first + place, target)
        columns.append(jnp.where(slot < counts[b][0:1], first[0:1] + slot, -1.0))
        first = first + counts[b]
    row = lax.broadcasted_iota(jnp.int32, (packed_rows, lanes), 0).astype(F32)
    packing = jnp.where(row == target[0:1], 1.0, 0.0).astype(BF16)
    incoming = jnp.concatenate([incoming_ref[b] for b in range(blocks)], axis=0)
    packed_ref[...] = jnp.dot(packing, incoming, preferred_element_type=F32).astype(BF16)
    column = jnp.concatenate(columns, axis=0)
    wide = spread_ref.shape[1]
    lane = lax.broadcasted_iota(jnp.int32, (blocks * CAP, wide), 1).astype(F32)
    column = jnp.concatenate([column] * (wide // 128), axis=1)
    spread_ref[...] = jnp.where(lane == column, 1.0, 0.0).astype(BF16)
    needed = jnp.max(first).astype(jnp.int32)
    budget = jnp.int32(0)
    for rows in BUDGETS[:-1]:
        budget = budget + (needed > rows).astype(jnp.int32)
    budget_ref[0] = budget


def pack(incoming):
    blocks, block_rows, width = incoming.shape
    rows = blocks * CAP
    vmem = pl.BlockSpec(memory_space=pltpu.VMEM)
    return pl.pallas_call(
        packing_kernel,
        out_shape=(
            jax.ShapeDtypeStruct((rows, width), BF16),
            jax.ShapeDtypeStruct((rows, blocks * block_rows), BF16),
            jax.ShapeDtypeStruct((1,), jnp.int32),
        ),
        in_specs=[vmem],
        out_specs=(vmem, vmem, pl.BlockSpec(memory_space=pltpu.SMEM)),
        compiler_params=pltpu.CompilerParams(vmem_limit_bytes=6 * 2**20),
        cost_estimate=pl.CostEstimate(flops=2 * rows * rows * width, bytes_accessed=6 * rows * width, transcendentals=0),
        name="pack",
    )(incoming)


def expert_kernel(
    cols_hbm, router_ref, up_hbm, down_hbm, part_hbm, terms_ref, cols, up, down, part, acc, sems
):
    tiles, rows, width = cols.shape
    pair = tiles // STEPS
    deep = pair * width

    def load_cols(c):
        return pltpu.make_async_copy(
            cols_hbm.at[pl.ds(c * pair, pair)], cols.at[pl.ds(c * pair, pair)], sems.at[0, c]
        )

    def load_up(c):
        return pltpu.make_async_copy(up_hbm.at[0, pl.ds(c * deep, deep)], up.at[c], sems.at[1, c])

    def load_down(c):
        return pltpu.make_async_copy(
            down_hbm.at[0, :, pl.ds(c * deep, deep)], down.at[c], sems.at[2, c]
        )

    def store_part(c):
        return pltpu.make_async_copy(
            part.at[pl.ds(c * pair, pair)], part_hbm.at[pl.ds(c * pair, pair)], sems.at[3, c]
        )

    for c in range(STEPS):
        load_cols(c).start()
        load_up(c).start()
    for c in range(STEPS):
        load_down(c).start()
    acc[...] = jnp.zeros_like(acc)

    def up_step(c, sums):
        squares, logits = sums
        load_cols(c).wait()
        load_up(c).wait()
        pieces = [cols[c * pair + i] for i in range(pair)]
        acc[...] += jnp.dot(
            jnp.concatenate(pieces, axis=1), up[c], preferred_element_type=F32
        )
        for i in range(pair):
            piece = pieces[i].astype(F32)
            squares = squares + jnp.sum(piece * piece, axis=1, keepdims=True)
            logits = logits + jnp.sum(
                piece * router_ref[pl.ds(c * pair + i, 1)], axis=1, keepdims=True
            )
        return squares, logits

    nothing = jnp.zeros((rows, 1), F32)
    squares, logits = lax.fori_loop(0, STEPS, up_step, (nothing, nothing))
    inv_rms = lax.rsqrt(squares / DM + 1e-06)
    up_sum = acc[...] * inv_rms
    hidden = (up_sum / (1.0 + jnp.exp(-up_sum))).astype(BF16)
    logit = logits * inv_rms
    high = logit.astype(BF16)
    rest = logit - high.astype(F32)
    middle = rest.astype(BF16)
    low = rest - middle.astype(F32)
    lane = lax.broadcasted_iota(jnp.int32, (rows, 128), 1)
    terms_ref[...] = jnp.where(
        lane == 0,
        high.astype(F32),
        jnp.where(lane == 1, middle.astype(F32), jnp.where(lane == 2, low, 0.0)),
    ).astype(BF16)

    def down_step(c, carry):
        load_down(c).wait()
        out = jnp.dot(hidden, down[c], preferred_element_type=F32).astype(BF16)
        for i in range(pair):
            part[c * pair + i] = out[:, i * width : (i + 1) * width]
        store_part(c).start()
        return carry

    lax.fori_loop(0, STEPS, down_step, 0)
    for c in range(STEPS):
        store_part(c).wait()


def expert(columns, own_router, up_weight, down_weight):
    tiles, rows, width = columns.shape
    hidden_units = up_weight.shape[2]
    deep = tiles // STEPS * width
    anywhere = pl.BlockSpec(memory_space=pl.ANY)
    vmem = pl.BlockSpec(memory_space=pltpu.VMEM)
    return pl.pallas_call(
        expert_kernel,
        out_shape=(
            jax.ShapeDtypeStruct((tiles, rows, width), BF16),
            jax.ShapeDtypeStruct((rows, 128), BF16),
        ),
        in_specs=[anywhere, vmem, anywhere, anywhere],
        out_specs=(anywhere, vmem),
        scratch_shapes=[
            pltpu.VMEM((tiles, rows, width), BF16),
            pltpu.VMEM((STEPS, deep, hidden_units), BF16),
            pltpu.VMEM((STEPS, hidden_units, deep), BF16),
            pltpu.VMEM((tiles, rows, width), BF16),
            pltpu.VMEM((rows, hidden_units), F32),
            pltpu.SemaphoreType.DMA((4, STEPS)),
        ],
        compiler_params=pltpu.CompilerParams(vmem_limit_bytes=40 * 2**20),
        cost_estimate=pl.CostEstimate(
            flops=4 * rows * tiles * width * hidden_units,
            bytes_accessed=4 * tiles * width * (hidden_units + rows),
            transcendentals=rows * hidden_units,
        ),
        name="expert",
    )(columns, own_router, up_weight, down_weight)


def local(
    mixer_input,
    gate_input,
    conv_state,
    conv_weight,
    conv_bias,
    state_proj,
    step_proj,
    step_bias,
    decay_rate,
    skip_gain,
    scan_state,
    output_proj,
    residual,
    router,
    expert_ids,
    active,
    up_weight,
    down_weight,
):
    n_tensor = lax.axis_size("tensor")
    experts_total = router.shape[1]
    sessions = expert_ids.shape[0]
    slice_width = residual.shape[1]
    low_rank = step_proj.shape[0]
    states = decay_rate.shape[0]

    live_float = active.astype(F32)
    live_mask = active == 1
    flat_ids = expert_ids.reshape(-1)
    flat_live = jnp.broadcast_to(live_mask[:, None], (sessions, 2)).reshape(-1)
    pairs = jnp.arange(flat_ids.shape[0], dtype=jnp.int32)
    earlier = (
        (flat_ids[:, None] == flat_ids[None, :])
        & (pairs[None, :] < pairs[:, None])
        & flat_live[None, :]
    )
    slot_index = jnp.sum(earlier.astype(jnp.int32), axis=1).reshape(sessions, 2)
    buffer_row = jnp.where(live_mask[:, None], expert_ids * CAP + slot_index, -1)
    row_numbers = jnp.arange(experts_total * CAP, dtype=jnp.int32)
    placement = jnp.any(buffer_row[None] == row_numbers[:, None, None], axis=2).astype(BF16)
    live_counts = jnp.sum(
        (flat_ids[None] == jnp.arange(experts_total, dtype=jnp.int32)[:, None]) & flat_live[None],
        axis=1,
    ).astype(BF16)

    window = jnp.concatenate([conv_state, mixer_input[:, None, :]], axis=1)
    conv_sum = jnp.sum(window.astype(F32) * conv_weight[None], axis=1) + conv_bias
    conv_out = jax.nn.silu(conv_sum).astype(BF16)
    partial_proj = jnp.dot(conv_out, state_proj, preferred_element_type=F32).astype(BF16)
    projected = sum_everywhere(partial_proj)
    step_raw = projected[:, :low_rank]
    input_map = projected[:, low_rank : low_rank + states]
    output_map = projected[:, low_rank + states :]
    step_norm = (
        step_raw * lax.rsqrt(jnp.mean(step_raw * step_raw, axis=1, keepdims=True) + 1e-06)
    ).astype(BF16)
    step_size = jax.nn.softplus(jnp.dot(step_norm, step_proj, preferred_element_type=F32) + step_bias)
    conv_float = conv_out.astype(F32)
    state_next = (
        jnp.exp(-step_size[:, None, :] * decay_rate[None]) * scan_state
        + (step_size * conv_float)[:, None, :] * input_map[:, :, None]
    )
    scan_out = jnp.sum(output_map[:, :, None] * state_next, axis=1) + skip_gain * conv_float
    gated = (scan_out * jax.nn.silu(gate_input.astype(F32)) * live_float[:, None]).astype(BF16)
    state_out = jnp.where(live_mask[:, None, None], state_next, scan_state)
    conv_cache = jnp.where(live_mask[:, None, None], window[:, 1:, :], conv_state)
    mixer_part = jnp.dot(gated, output_proj, preferred_element_type=F32).astype(BF16)
    hidden_local = sum_over_tensor(
        mixer_part.reshape(sessions, n_tensor, slice_width).transpose(1, 0, 2)
    ) + residual.astype(F32)

    outgoing = jnp.dot(placement, hidden_local.astype(BF16), preferred_element_type=F32).astype(BF16)
    outgoing = jnp.concatenate(
        [
            outgoing.reshape(experts_total, CAP, slice_width),
            jnp.broadcast_to(live_counts[:, None, None], (experts_total, 8, slice_width)),
        ],
        axis=1,
    )
    incoming = lax.all_to_all(outgoing, "dp", split_axis=0, concat_axis=0, tiled=True)
    packed, spread, budget = pack(incoming)
    own_router = lax.dynamic_slice_in_dim(router, lax.axis_index("dp"), 1, 1)[:, 0]
    own_router = own_router.astype(F32).reshape(n_tensor, slice_width)

    def on_rows(rows):
        def run(packed, spread, own_router, up_weight, down_weight):
            columns = lax.all_to_all(
                jnp.broadcast_to(packed[None, :rows], (n_tensor, rows, slice_width)),
                "tensor",
                split_axis=0,
                concat_axis=0,
                tiled=True,
            )
            expert_part, terms = expert(columns, own_router, up_weight, down_weight)
            share = jnp.concatenate([sum_over_tensor(expert_part).astype(BF16), terms], axis=1)
            return jnp.dot(spread[:, :rows], share, preferred_element_type=F32).astype(BF16)

        return run

    replies = lax.switch(
        budget[0], [on_rows(rows) for rows in BUDGETS], packed, spread, own_router, up_weight, down_weight
    )

    returned = lax.all_to_all(
        replies.reshape(experts_total, CAP, slice_width + 128),
        "dp",
        split_axis=0,
        concat_axis=0,
        tiled=True,
    ).reshape(experts_total * CAP, slice_width + 128)
    chosen = buffer_row.reshape(-1)[:, None] == row_numbers[None]
    gathered = jnp.dot(chosen.astype(BF16), returned, preferred_element_type=F32).reshape(
        sessions, 2, slice_width + 128
    )
    chosen_logit = gathered[:, :, slice_width] + (
        gathered[:, :, slice_width + 1] + gathered[:, :, slice_width + 2]
    )
    first = 1.0 / (1.0 + jnp.exp(chosen_logit[:, 1] - chosen_logit[:, 0]))
    second = 1.0 / (1.0 + jnp.exp(chosen_logit[:, 0] - chosen_logit[:, 1]))
    route_weight = jnp.stack([first, second], axis=1) * live_float[:, None]
    layer_out = (hidden_local + jnp.sum(route_weight[:, :, None] * gathered[:, :, :slice_width], axis=1)).astype(BF16)
    return (layer_out, state_out, conv_cache)


def solution(mesh):
    placed = (
        P("dp", "tensor"),
        P("dp", "tensor"),
        P("dp", None, "tensor"),
        P(None, "tensor"),
        P("tensor"),
        P("tensor", None),
        P(None, "tensor"),
        P("tensor"),
        P(None, "tensor"),
        P("tensor"),
        P("dp", None, "tensor"),
        P("tensor", None),
        P("dp", "tensor"),
        P(),
        P("dp", None),
        P("dp"),
        P("dp", None, "tensor"),
        P("dp", "tensor", None),
    )
    return jax.shard_map(
        local,
        mesh=mesh,
        in_specs=placed,
        out_specs=(P("dp", "tensor"), P("dp", None, "tensor"), P("dp", None, "tensor")),
        check_vma=False,
    )
```

```python
import math

import jax
import jax.numpy as jnp
from jax import lax
from jax.experimental import pallas as pl
from jax.experimental.pallas import tpu as pltpu
from jax.sharding import PartitionSpec as P

DM = 4096
CAP = 40
F32 = jnp.float32
BF16 = jnp.bfloat16
STEPS = 4
STRAIGHT = 256
BUDGETS = (64, 80, 96, 112, 128, 144, 160, 192, 224, 256, 320)


def sum_over_tensor(pieces):
    return jnp.sum(
        lax.all_to_all(pieces, "tensor", split_axis=0, concat_axis=0, tiled=True).astype(F32), axis=0
    )


def sum_everywhere(piece):
    count = lax.axis_size("tensor")
    side = math.isqrt(count)
    for along_z in (True, False):
        total = piece.astype(F32)
        for step in range(1, side):
            ring = []
            for i in range(count):
                z, x = i // side, i % side
                if along_z:
                    z = (z + step) % side
                else:
                    x = (x + step) % side
                ring.append((i, z * side + x))
            total = total + lax.ppermute(piece, "tensor", ring).astype(F32)
        piece = total.astype(BF16)
    return total


def packing_kernel(incoming_ref, packed_ref, spread_ref, budget_ref):
    blocks, block_rows, width = incoming_ref.shape
    packed_rows = packed_ref.shape[0]
    counts = [incoming_ref[b].astype(F32)[CAP:, :128] for b in range(blocks)]
    lanes = blocks * block_rows
    lane = lax.broadcasted_iota(jnp.int32, (8, lanes), 1).astype(F32)
    slot = lax.broadcasted_iota(jnp.int32, (CAP, 128), 0).astype(F32)
    target = jnp.full((8, lanes), -1.0, F32)
    first = jnp.zeros((8, 128), F32)
    columns = []
    for b in range(blocks):
        wide_count = jnp.concatenate([counts[b]] * (lanes // 128), axis=1)
        wide_first = jnp.concatenate([first] * (lanes // 128), axis=1)
        place = lane - b * block_rows
        target = jnp.where((place >= 0) & (place < wide_count), wide_first + place, target)
        columns.append(jnp.where(slot < counts[b][0:1], first[0:1] + slot, -1.0))
        first = first + counts[b]
    row = lax.broadcasted_iota(jnp.int32, (packed_rows, lanes), 0).astype(F32)
    packing = jnp.where(row == target[0:1], 1.0, 0.0).astype(BF16)
    incoming = jnp.concatenate([incoming_ref[b] for b in range(blocks)], axis=0)
    packed_ref[...] = jnp.dot(packing, incoming, preferred_element_type=F32).astype(BF16)
    column = jnp.concatenate(columns, axis=0)
    wide = spread_ref.shape[1]
    lane = lax.broadcasted_iota(jnp.int32, (blocks * CAP, wide), 1).astype(F32)
    column = jnp.concatenate([column] * (wide // 128), axis=1)
    spread_ref[...] = jnp.where(lane == column, 1.0, 0.0).astype(BF16)
    needed = jnp.max(first).astype(jnp.int32)
    budget = jnp.int32(0)
    for rows in BUDGETS[:-1]:
        budget = budget + (needed > rows).astype(jnp.int32)
    budget_ref[0] = budget


def pack(incoming):
    blocks, block_rows, width = incoming.shape
    rows = blocks * CAP
    vmem = pl.BlockSpec(memory_space=pltpu.VMEM)
    return pl.pallas_call(
        packing_kernel,
        out_shape=(
            jax.ShapeDtypeStruct((rows, width), BF16),
            jax.ShapeDtypeStruct((rows, blocks * block_rows), BF16),
            jax.ShapeDtypeStruct((1,), jnp.int32),
        ),
        in_specs=[vmem],
        out_specs=(vmem, vmem, pl.BlockSpec(memory_space=pltpu.SMEM)),
        compiler_params=pltpu.CompilerParams(vmem_limit_bytes=6 * 2**20),
        cost_estimate=pl.CostEstimate(flops=2 * rows * rows * width, bytes_accessed=6 * rows * width, transcendentals=0),
        name="pack",
    )(incoming)


def expert_kernel(
    cols_hbm, router_ref, up_hbm, down_hbm, part_hbm, terms_ref, cols, up, down, part, acc, sems
):
    tiles, rows, width = cols.shape
    pair = tiles // STEPS
    deep = pair * width

    def load_cols(c):
        return pltpu.make_async_copy(
            cols_hbm.at[pl.ds(c * pair, pair)], cols.at[pl.ds(c * pair, pair)], sems.at[0, c]
        )

    def load_up(c):
        return pltpu.make_async_copy(up_hbm.at[0, pl.ds(c * deep, deep)], up.at[c], sems.at[1, c])

    def load_down(c):
        return pltpu.make_async_copy(
            down_hbm.at[0, :, pl.ds(c * deep, deep)], down.at[c], sems.at[2, c]
        )

    def store_part(c):
        return pltpu.make_async_copy(
            part.at[pl.ds(c * pair, pair)], part_hbm.at[pl.ds(c * pair, pair)], sems.at[3, c]
        )

    for c in range(STEPS):
        load_cols(c).start()
        load_up(c).start()
    for c in range(STEPS):
        load_down(c).start()
    squares = jnp.zeros((rows, 1), F32)
    logits = jnp.zeros((rows, 1), F32)
    straight = rows >= STRAIGHT
    acc[...] = jnp.zeros_like(acc)

    def up_step(c, sums):
        squares, logits = sums
        load_cols(c).wait()
        load_up(c).wait()
        pieces = [cols[c * pair + i] for i in range(pair)]
        acc[...] += jnp.dot(jnp.concatenate(pieces, axis=1), up[c], preferred_element_type=F32)
        for i in range(pair):
            piece = pieces[i].astype(F32)
            squares = squares + jnp.sum(piece * piece, axis=1, keepdims=True)
            logits = logits + jnp.sum(
                piece * router_ref[pl.ds(c * pair + i, 1)], axis=1, keepdims=True
            )
        return squares, logits

    squares, logits = lax.fori_loop(0, STEPS, up_step, (squares, logits), unroll=straight)
    inv_rms = lax.rsqrt(squares / DM + 1e-06)
    up_sum = acc[...] * inv_rms
    hidden = (up_sum / (1.0 + jnp.exp(-up_sum))).astype(BF16)
    logit = logits * inv_rms
    high = logit.astype(BF16)
    rest = logit - high.astype(F32)
    middle = rest.astype(BF16)
    low = rest - middle.astype(F32)
    lane = lax.broadcasted_iota(jnp.int32, (rows, 128), 1)
    terms_ref[...] = jnp.where(
        lane == 0,
        high.astype(F32),
        jnp.where(lane == 1, middle.astype(F32), jnp.where(lane == 2, low, 0.0)),
    ).astype(BF16)

    def down_step(c, carry):
        load_down(c).wait()
        out = jnp.dot(hidden, down[c], preferred_element_type=F32).astype(BF16)
        for i in range(pair):
            part[c * pair + i] = out[:, i * width : (i + 1) * width]
        store_part(c).start()
        return carry

    lax.fori_loop(0, STEPS, down_step, 0, unroll=straight)
    for c in range(STEPS):
        store_part(c).wait()


def expert(columns, own_router, up_weight, down_weight):
    tiles, rows, width = columns.shape
    hidden_units = up_weight.shape[2]
    deep = tiles // STEPS * width
    anywhere = pl.BlockSpec(memory_space=pl.ANY)
    far = pl.BlockSpec(memory_space=pltpu.HBM)
    vmem = pl.BlockSpec(memory_space=pltpu.VMEM)
    return pl.pallas_call(
        expert_kernel,
        out_shape=(
            jax.ShapeDtypeStruct((tiles, rows, width), BF16),
            jax.ShapeDtypeStruct((rows, 128), BF16),
        ),
        in_specs=[anywhere, vmem, far, far],
        out_specs=(anywhere, vmem),
        scratch_shapes=[
            pltpu.VMEM((tiles, rows, width), BF16),
            pltpu.VMEM((STEPS, deep, hidden_units), BF16),
            pltpu.VMEM((STEPS, hidden_units, deep), BF16),
            pltpu.VMEM((tiles, rows, width), BF16),
            pltpu.VMEM((rows, hidden_units), F32),
            pltpu.SemaphoreType.DMA((4, STEPS)),
        ],
        compiler_params=pltpu.CompilerParams(vmem_limit_bytes=40 * 2**20),
        cost_estimate=pl.CostEstimate(
            flops=4 * rows * tiles * width * hidden_units,
            bytes_accessed=4 * tiles * width * (hidden_units + rows),
            transcendentals=rows * hidden_units,
        ),
        name="expert",
    )(columns, own_router, up_weight, down_weight)


def local(
    mixer_input,
    gate_input,
    conv_state,
    conv_weight,
    conv_bias,
    state_proj,
    step_proj,
    step_bias,
    decay_rate,
    skip_gain,
    scan_state,
    output_proj,
    residual,
    router,
    expert_ids,
    active,
    up_weight,
    down_weight,
):
    n_tensor = lax.axis_size("tensor")
    experts_total = router.shape[1]
    sessions = expert_ids.shape[0]
    slice_width = residual.shape[1]
    low_rank = step_proj.shape[0]
    states = decay_rate.shape[0]

    live_float = active.astype(F32)
    live_mask = active == 1
    flat_ids = expert_ids.reshape(-1)
    flat_live = jnp.broadcast_to(live_mask[:, None], (sessions, 2)).reshape(-1)
    pairs = jnp.arange(flat_ids.shape[0], dtype=jnp.int32)
    earlier = (
        (flat_ids[:, None] == flat_ids[None, :])
        & (pairs[None, :] < pairs[:, None])
        & flat_live[None, :]
    )
    slot_index = jnp.sum(earlier.astype(jnp.int32), axis=1).reshape(sessions, 2)
    buffer_row = jnp.where(live_mask[:, None], expert_ids * CAP + slot_index, -1)
    row_numbers = jnp.arange(experts_total * CAP, dtype=jnp.int32)
    placement = jnp.any(buffer_row[None] == row_numbers[:, None, None], axis=2).astype(BF16)
    live_counts = jnp.sum(
        (flat_ids[None] == jnp.arange(experts_total, dtype=jnp.int32)[:, None]) & flat_live[None],
        axis=1,
    ).astype(BF16)

    window = jnp.concatenate([conv_state, mixer_input[:, None, :]], axis=1)
    conv_sum = jnp.sum(window.astype(F32) * conv_weight[None], axis=1) + conv_bias
    conv_out = jax.nn.silu(conv_sum).astype(BF16)
    partial_proj = jnp.dot(conv_out, state_proj, preferred_element_type=F32).astype(BF16)
    projected = sum_everywhere(partial_proj)
    step_raw = projected[:, :low_rank]
    input_map = projected[:, low_rank : low_rank + states]
    output_map = projected[:, low_rank + states :]
    step_norm = (
        step_raw * lax.rsqrt(jnp.mean(step_raw * step_raw, axis=1, keepdims=True) + 1e-06)
    ).astype(BF16)
    step_size = jax.nn.softplus(jnp.dot(step_norm, step_proj, preferred_element_type=F32) + step_bias)
    conv_float = conv_out.astype(F32)
    state_next = (
        jnp.exp(-step_size[:, None, :] * decay_rate[None]) * scan_state
        + (step_size * conv_float)[:, None, :] * input_map[:, :, None]
    )
    scan_out = jnp.sum(output_map[:, :, None] * state_next, axis=1) + skip_gain * conv_float
    gated = (scan_out * jax.nn.silu(gate_input.astype(F32)) * live_float[:, None]).astype(BF16)
    state_out = jnp.where(live_mask[:, None, None], state_next, scan_state)
    conv_cache = jnp.where(live_mask[:, None, None], window[:, 1:, :], conv_state)
    mixer_part = jnp.dot(gated, output_proj, preferred_element_type=F32).astype(BF16)
    hidden_local = sum_over_tensor(
        mixer_part.reshape(sessions, n_tensor, slice_width).transpose(1, 0, 2)
    ) + residual.astype(F32)

    outgoing = jnp.dot(placement, hidden_local.astype(BF16), preferred_element_type=F32).astype(BF16)
    outgoing = jnp.concatenate(
        [
            outgoing.reshape(experts_total, CAP, slice_width),
            jnp.broadcast_to(live_counts[:, None, None], (experts_total, 8, slice_width)),
        ],
        axis=1,
    )
    incoming = lax.all_to_all(outgoing, "dp", split_axis=0, concat_axis=0, tiled=True)
    packed, spread, budget = pack(incoming)
    own_router = lax.dynamic_slice_in_dim(router, lax.axis_index("dp"), 1, 1)[:, 0]
    own_router = own_router.astype(F32).reshape(n_tensor, slice_width)

    def on_rows(rows):
        def run(packed, spread, own_router, up_weight, down_weight):
            columns = lax.all_to_all(
                jnp.broadcast_to(packed[None, :rows], (n_tensor, rows, slice_width)),
                "tensor",
                split_axis=0,
                concat_axis=0,
                tiled=True,
            )
            expert_part, terms = expert(columns, own_router, up_weight, down_weight)
            share = jnp.concatenate([sum_over_tensor(expert_part).astype(BF16), terms], axis=1)
            return jnp.dot(spread[:, :rows], share, preferred_element_type=F32).astype(BF16)

        return run

    replies = lax.switch(
        budget[0], [on_rows(rows) for rows in BUDGETS], packed, spread, own_router, up_weight, down_weight
    )

    returned = lax.all_to_all(
        replies.reshape(experts_total, CAP, slice_width + 128),
        "dp",
        split_axis=0,
        concat_axis=0,
        tiled=True,
    ).reshape(experts_total * CAP, slice_width + 128)
    chosen = buffer_row.reshape(-1)[:, None] == row_numbers[None]
    gathered = jnp.dot(chosen.astype(BF16), returned, preferred_element_type=F32).reshape(
        sessions, 2, slice_width + 128
    )
    chosen_logit = gathered[:, :, slice_width] + (
        gathered[:, :, slice_width + 1] + gathered[:, :, slice_width + 2]
    )
    first = 1.0 / (1.0 + jnp.exp(chosen_logit[:, 1] - chosen_logit[:, 0]))
    second = 1.0 / (1.0 + jnp.exp(chosen_logit[:, 0] - chosen_logit[:, 1]))
    route_weight = jnp.stack([first, second], axis=1) * live_float[:, None]
    layer_out = (hidden_local + jnp.sum(route_weight[:, :, None] * gathered[:, :, :slice_width], axis=1)).astype(BF16)
    return (layer_out, state_out, conv_cache)


def solution(mesh):
    placed = (
        P("dp", "tensor"),
        P("dp", "tensor"),
        P("dp", None, "tensor"),
        P(None, "tensor"),
        P("tensor"),
        P("tensor", None),
        P(None, "tensor"),
        P("tensor"),
        P(None, "tensor"),
        P("tensor"),
        P("dp", None, "tensor"),
        P("tensor", None),
        P("dp", "tensor"),
        P(),
        P("dp", None),
        P("dp"),
        P("dp", None, "tensor"),
        P("dp", "tensor", None),
    )
    return jax.shard_map(
        local,
        mesh=mesh,
        in_specs=placed,
        out_specs=(P("dp", "tensor"), P("dp", None, "tensor"), P("dp", None, "tensor")),
        check_vma=False,
    )
```

```python
import math

import jax
import jax.numpy as jnp
from jax import lax
from jax.experimental import pallas as pl
from jax.experimental.pallas import tpu as pltpu
from jax.sharding import PartitionSpec as P

DM = 4096
CAP = 40
F32 = jnp.float32
BF16 = jnp.bfloat16
STEPS = 4
BUDGETS = (64, 96, 128, 160, 192, 256, 320)
STRIDE = 48


def sum_over_tensor(pieces):
    return jnp.sum(
        lax.all_to_all(pieces, "tensor", split_axis=0, concat_axis=0, tiled=True).astype(F32), axis=0
    )


def sum_everywhere(piece):
    count = lax.axis_size("tensor")
    side = math.isqrt(count)
    for along_z in (True, False):
        total = piece.astype(F32)
        for step in range(1, side):
            ring = []
            for i in range(count):
                z, x = i // side, i % side
                if along_z:
                    z = (z + step) % side
                else:
                    x = (x + step) % side
                ring.append((i, z * side + x))
            total = total + lax.ppermute(piece, "tensor", ring).astype(F32)
        piece = total.astype(BF16)
    return total


def packing_kernel(incoming_ref, packed_ref, spread_ref, budget_ref):
    blocks, block_rows, width = incoming_ref.shape
    packed_rows = packed_ref.shape[0]
    counts = [incoming_ref[b].astype(F32)[CAP:, :128] for b in range(blocks)]
    lanes = blocks * block_rows
    lane = lax.broadcasted_iota(jnp.int32, (8, lanes), 1).astype(F32)
    slot = lax.broadcasted_iota(jnp.int32, (CAP, 128), 0).astype(F32)
    target = jnp.full((8, lanes), -1.0, F32)
    first = jnp.zeros((8, 128), F32)
    columns = []
    for b in range(blocks):
        wide_count = jnp.concatenate([counts[b]] * (lanes // 128), axis=1)
        wide_first = jnp.concatenate([first] * (lanes // 128), axis=1)
        place = lane - b * block_rows
        target = jnp.where((place >= 0) & (place < wide_count), wide_first + place, target)
        columns.append(jnp.where(slot < counts[b][0:1], first[0:1] + slot, -1.0))
        first = first + counts[b]
    row = lax.broadcasted_iota(jnp.int32, (packed_rows, lanes), 0).astype(F32)
    packing = jnp.where(row == target[0:1], 1.0, 0.0).astype(BF16)
    incoming = jnp.concatenate([incoming_ref[b] for b in range(blocks)], axis=0)
    packed_ref[...] = jnp.dot(packing, incoming, preferred_element_type=F32).astype(BF16)
    column = jnp.concatenate(columns, axis=0)
    wide = spread_ref.shape[1]
    lane = lax.broadcasted_iota(jnp.int32, (blocks * CAP, wide), 1).astype(F32)
    column = jnp.concatenate([column] * (wide // 128), axis=1)
    spread_ref[...] = jnp.where(lane == column, 1.0, 0.0).astype(BF16)
    needed = jnp.max(first).astype(jnp.int32)
    budget = jnp.int32(0)
    for rows in BUDGETS[:-1]:
        budget = budget + (needed > rows).astype(jnp.int32)
    budget_ref[0] = budget


def pack(incoming):
    blocks, block_rows, width = incoming.shape
    rows = blocks * CAP
    vmem = pl.BlockSpec(memory_space=pltpu.VMEM)
    return pl.pallas_call(
        packing_kernel,
        out_shape=(
            jax.ShapeDtypeStruct((rows, width), BF16),
            jax.ShapeDtypeStruct((rows, blocks * block_rows), BF16),
            jax.ShapeDtypeStruct((1,), jnp.int32),
        ),
        in_specs=[vmem],
        out_specs=(vmem, vmem, pl.BlockSpec(memory_space=pltpu.SMEM)),
        compiler_params=pltpu.CompilerParams(vmem_limit_bytes=6 * 2**20),
        cost_estimate=pl.CostEstimate(flops=2 * rows * rows * width, bytes_accessed=6 * rows * width, transcendentals=0),
        name="pack",
    )(incoming)


def expert_kernel(
    cols_hbm, router_ref, up_hbm, down_hbm, part_hbm, terms_ref, cols, up, down, part, acc, sems
):
    tiles, rows, width = cols.shape
    pair = tiles // STEPS
    deep = pair * width

    def load_cols(c):
        return pltpu.make_async_copy(
            cols_hbm.at[pl.ds(c * pair, pair)], cols.at[pl.ds(c * pair, pair)], sems.at[0, c]
        )

    def load_up(c):
        return pltpu.make_async_copy(up_hbm.at[0, pl.ds(c * deep, deep)], up.at[c], sems.at[1, c])

    def load_down(c):
        return pltpu.make_async_copy(
            down_hbm.at[0, :, pl.ds(c * deep, deep)], down.at[c], sems.at[2, c]
        )

    def store_part(c):
        return pltpu.make_async_copy(
            part.at[pl.ds(c * pair, pair)], part_hbm.at[pl.ds(c * pair, pair)], sems.at[3, c]
        )

    for c in range(STEPS):
        load_cols(c).start()
        load_up(c).start()
    for c in range(STEPS):
        load_down(c).start()
    squares = jnp.zeros((rows, 1), F32)
    logits = jnp.zeros((rows, 1), F32)
    acc[...] = jnp.zeros_like(acc)

    def up_step(c, sums):
        squares, logits = sums
        load_cols(c).wait()
        load_up(c).wait()
        pieces = [cols[c * pair + i] for i in range(pair)]
        acc[...] += jnp.dot(jnp.concatenate(pieces, axis=1), up[c], preferred_element_type=F32)
        for i in range(pair):
            piece = pieces[i].astype(F32)
            squares = squares + jnp.sum(piece * piece, axis=1, keepdims=True)
            logits = logits + jnp.sum(
                piece * router_ref[pl.ds(c * pair + i, 1)], axis=1, keepdims=True
            )
        return squares, logits

    squares, logits = lax.fori_loop(0, STEPS, up_step, (squares, logits))
    inv_rms = lax.rsqrt(squares / DM + 1e-06)
    up_sum = acc[...] * inv_rms
    hidden = (up_sum / (1.0 + jnp.exp(-up_sum))).astype(BF16)
    logit = logits * inv_rms
    high = logit.astype(BF16)
    rest = logit - high.astype(F32)
    middle = rest.astype(BF16)
    low = rest - middle.astype(F32)
    lane = lax.broadcasted_iota(jnp.int32, (rows, 128), 1)
    terms_ref[...] = jnp.where(
        lane == 0,
        high.astype(F32),
        jnp.where(lane == 1, middle.astype(F32), jnp.where(lane == 2, low, 0.0)),
    ).astype(BF16)

    def down_step(c, carry):
        load_down(c).wait()
        out = jnp.dot(hidden, down[c], preferred_element_type=F32).astype(BF16)
        for i in range(pair):
            part[c * pair + i] = out[:, i * width : (i + 1) * width]
        store_part(c).start()
        return carry

    lax.fori_loop(0, STEPS, down_step, 0)
    for c in range(STEPS):
        store_part(c).wait()


def expert(columns, own_router, up_weight, down_weight):
    tiles, rows, width = columns.shape
    hidden_units = up_weight.shape[2]
    deep = tiles // STEPS * width
    anywhere = pl.BlockSpec(memory_space=pl.ANY)
    far = pl.BlockSpec(memory_space=pltpu.HBM)
    vmem = pl.BlockSpec(memory_space=pltpu.VMEM)
    return pl.pallas_call(
        expert_kernel,
        out_shape=(
            jax.ShapeDtypeStruct((tiles, rows, width), BF16),
            jax.ShapeDtypeStruct((rows, 128), BF16),
        ),
        in_specs=[anywhere, vmem, far, far],
        out_specs=(anywhere, vmem),
        scratch_shapes=[
            pltpu.VMEM((tiles, rows, width), BF16),
            pltpu.VMEM((STEPS, deep, hidden_units), BF16),
            pltpu.VMEM((STEPS, hidden_units, deep), BF16),
            pltpu.VMEM((tiles, rows, width), BF16),
            pltpu.VMEM((rows, hidden_units), F32),
            pltpu.SemaphoreType.DMA((4, STEPS)),
        ],
        compiler_params=pltpu.CompilerParams(vmem_limit_bytes=40 * 2**20),
        cost_estimate=pl.CostEstimate(
            flops=4 * rows * tiles * width * hidden_units,
            bytes_accessed=4 * tiles * width * (hidden_units + rows),
            transcendentals=rows * hidden_units,
        ),
        name="expert",
    )(columns, own_router, up_weight, down_weight)


def local(
    mixer_input,
    gate_input,
    conv_state,
    conv_weight,
    conv_bias,
    state_proj,
    step_proj,
    step_bias,
    decay_rate,
    skip_gain,
    scan_state,
    output_proj,
    residual,
    router,
    expert_ids,
    active,
    up_weight,
    down_weight,
):
    n_tensor = lax.axis_size("tensor")
    experts_total = router.shape[1]
    sessions = expert_ids.shape[0]
    slice_width = residual.shape[1]
    low_rank = step_proj.shape[0]
    states = decay_rate.shape[0]

    live_float = active.astype(F32)
    live_mask = active == 1
    flat_ids = expert_ids.reshape(-1)
    flat_live = jnp.broadcast_to(live_mask[:, None], (sessions, 2)).reshape(-1)
    pairs = jnp.arange(flat_ids.shape[0], dtype=jnp.int32)
    earlier = (
        (flat_ids[:, None] == flat_ids[None, :])
        & (pairs[None, :] < pairs[:, None])
        & flat_live[None, :]
    )
    slot_index = jnp.sum(earlier.astype(jnp.int32), axis=1).reshape(sessions, 2)
    buffer_row = jnp.where(live_mask[:, None], expert_ids * CAP + slot_index, -1)
    row_numbers = jnp.arange(experts_total * CAP, dtype=jnp.int32)
    out_numbers = jnp.arange(experts_total * STRIDE, dtype=jnp.int32)
    out_row = jnp.where(live_mask[:, None], expert_ids * STRIDE + slot_index, -1)
    placement = jnp.any(out_row[None] == out_numbers[:, None, None], axis=2)
    counting = (out_numbers[:, None] // STRIDE == jnp.arange(experts_total, dtype=jnp.int32)[None]) & (
        out_numbers[:, None] % STRIDE >= CAP
    )
    placement = jnp.concatenate([placement, counting], axis=1).astype(BF16)
    live_counts = jnp.sum(
        (flat_ids[None] == jnp.arange(experts_total, dtype=jnp.int32)[:, None]) & flat_live[None],
        axis=1,
    ).astype(BF16)

    window = jnp.concatenate([conv_state, mixer_input[:, None, :]], axis=1)
    conv_sum = jnp.sum(window.astype(F32) * conv_weight[None], axis=1) + conv_bias
    conv_out = jax.nn.silu(conv_sum).astype(BF16)
    partial_proj = jnp.dot(conv_out, state_proj, preferred_element_type=F32).astype(BF16)
    projected = sum_everywhere(partial_proj)
    step_raw = projected[:, :low_rank]
    input_map = projected[:, low_rank : low_rank + states]
    output_map = projected[:, low_rank + states :]
    step_norm = (
        step_raw * lax.rsqrt(jnp.mean(step_raw * step_raw, axis=1, keepdims=True) + 1e-06)
    ).astype(BF16)
    step_size = jax.nn.softplus(jnp.dot(step_norm, step_proj, preferred_element_type=F32) + step_bias)
    conv_float = conv_out.astype(F32)
    state_next = (
        jnp.exp(-step_size[:, None, :] * decay_rate[None]) * scan_state
        + (step_size * conv_float)[:, None, :] * input_map[:, :, None]
    )
    scan_out = jnp.sum(output_map[:, :, None] * state_next, axis=1) + skip_gain * conv_float
    gated = (scan_out * jax.nn.silu(gate_input.astype(F32)) * live_float[:, None]).astype(BF16)
    state_out = jnp.where(live_mask[:, None, None], state_next, scan_state)
    conv_cache = jnp.where(live_mask[:, None, None], window[:, 1:, :], conv_state)
    mixer_part = jnp.dot(gated, output_proj, preferred_element_type=F32).astype(BF16)
    hidden_local = sum_over_tensor(
        mixer_part.reshape(sessions, n_tensor, slice_width).transpose(1, 0, 2)
    ) + residual.astype(F32)

    sources = jnp.concatenate(
        [
            hidden_local.astype(BF16),
            jnp.broadcast_to(live_counts[:, None], (experts_total, slice_width)),
        ],
        axis=0,
    )
    outgoing = jnp.dot(placement, sources, preferred_element_type=F32).astype(BF16)
    outgoing = outgoing.reshape(experts_total, STRIDE, slice_width)
    incoming = lax.all_to_all(outgoing, "dp", split_axis=0, concat_axis=0, tiled=True)
    packed, spread, budget = pack(incoming)
    own_router = lax.dynamic_slice_in_dim(router, lax.axis_index("dp"), 1, 1)[:, 0]
    own_router = own_router.astype(F32).reshape(n_tensor, slice_width)

    def on_rows(rows):
        def run(packed, spread, own_router, up_weight, down_weight):
            columns = lax.all_to_all(
                jnp.broadcast_to(packed[None, :rows], (n_tensor, rows, slice_width)),
                "tensor",
                split_axis=0,
                concat_axis=0,
                tiled=True,
            )
            expert_part, terms = expert(columns, own_router, up_weight, down_weight)
            share = jnp.concatenate([sum_over_tensor(expert_part).astype(BF16), terms], axis=1)
            return jnp.dot(spread[:, :rows], share, preferred_element_type=F32).astype(BF16)

        return run

    replies = lax.switch(
        budget[0], [on_rows(rows) for rows in BUDGETS], packed, spread, own_router, up_weight, down_weight
    )

    returned = lax.all_to_all(
        replies.reshape(experts_total, CAP, slice_width + 128),
        "dp",
        split_axis=0,
        concat_axis=0,
        tiled=True,
    ).reshape(experts_total * CAP, slice_width + 128)
    chosen = buffer_row.reshape(-1)[:, None] == row_numbers[None]
    gathered = jnp.dot(chosen.astype(BF16), returned, preferred_element_type=F32).reshape(
        sessions, 2, slice_width + 128
    )
    chosen_logit = gathered[:, :, slice_width] + (
        gathered[:, :, slice_width + 1] + gathered[:, :, slice_width + 2]
    )
    first = 1.0 / (1.0 + jnp.exp(chosen_logit[:, 1] - chosen_logit[:, 0]))
    second = 1.0 / (1.0 + jnp.exp(chosen_logit[:, 0] - chosen_logit[:, 1]))
    route_weight = jnp.stack([first, second], axis=1) * live_float[:, None]
    layer_out = (hidden_local + jnp.sum(route_weight[:, :, None] * gathered[:, :, :slice_width], axis=1)).astype(BF16)
    return (layer_out, state_out, conv_cache)


def solution(mesh):
    placed = (
        P("dp", "tensor"),
        P("dp", "tensor"),
        P("dp", None, "tensor"),
        P(None, "tensor"),
        P("tensor"),
        P("tensor", None),
        P(None, "tensor"),
        P("tensor"),
        P(None, "tensor"),
        P("tensor"),
        P("dp", None, "tensor"),
        P("tensor", None),
        P("dp", "tensor"),
        P(),
        P("dp", None),
        P("dp"),
        P("dp", None, "tensor"),
        P("dp", "tensor", None),
    )
    return jax.shard_map(
        local,
        mesh=mesh,
        in_specs=placed,
        out_specs=(P("dp", "tensor"), P("dp", None, "tensor"), P("dp", None, "tensor")),
        check_vma=False,
    )
```

```python
import math

import jax
import jax.numpy as jnp
from jax import lax
from jax.experimental import pallas as pl
from jax.experimental.pallas import tpu as pltpu
from jax.sharding import PartitionSpec as P

DM = 4096
CAP = 40
F32 = jnp.float32
BF16 = jnp.bfloat16
STEPS = 4
BUDGETS = (48, 64, 80, 96, 128, 192, 256, 320)
STRIDE = 48


def sum_over_tensor(pieces):
    return jnp.sum(
        lax.all_to_all(pieces, "tensor", split_axis=0, concat_axis=0, tiled=True).astype(F32), axis=0
    )


def sum_everywhere(piece):
    count = lax.axis_size("tensor")
    side = math.isqrt(count)
    for along_z in (True, False):
        total = piece.astype(F32)
        for step in range(1, side):
            ring = []
            for i in range(count):
                z, x = i // side, i % side
                if along_z:
                    z = (z + step) % side
                else:
                    x = (x + step) % side
                ring.append((i, z * side + x))
            total = total + lax.ppermute(piece, "tensor", ring).astype(F32)
        piece = total.astype(BF16)
    return total


def packing_kernel(incoming_ref, packed_ref, spread_ref, budget_ref):
    blocks, block_rows, width = incoming_ref.shape
    packed_rows = packed_ref.shape[0]
    counts = [incoming_ref[b].astype(F32)[CAP:, :128] for b in range(blocks)]
    lanes = blocks * block_rows
    lane = lax.broadcasted_iota(jnp.int32, (8, lanes), 1).astype(F32)
    slot = lax.broadcasted_iota(jnp.int32, (CAP, 128), 0).astype(F32)
    target = jnp.full((8, lanes), -1.0, F32)
    first = jnp.zeros((8, 128), F32)
    columns = []
    for b in range(blocks):
        wide_count = jnp.concatenate([counts[b]] * (lanes // 128), axis=1)
        wide_first = jnp.concatenate([first] * (lanes // 128), axis=1)
        place = lane - b * block_rows
        target = jnp.where((place >= 0) & (place < wide_count), wide_first + place, target)
        columns.append(jnp.where(slot < counts[b][0:1], first[0:1] + slot, -1.0))
        first = first + counts[b]
    row = lax.broadcasted_iota(jnp.int32, (packed_rows, lanes), 0).astype(F32)
    packing = jnp.where(row == target[0:1], 1.0, 0.0).astype(BF16)
    incoming = jnp.concatenate([incoming_ref[b] for b in range(blocks)], axis=0)
    packed_ref[...] = jnp.dot(packing, incoming, preferred_element_type=F32).astype(BF16)
    column = jnp.concatenate(columns, axis=0)
    wide = spread_ref.shape[1]
    lane = lax.broadcasted_iota(jnp.int32, (blocks * CAP, wide), 1).astype(F32)
    column = jnp.concatenate([column] * (wide // 128), axis=1)
    spread_ref[...] = jnp.where(lane == column, 1.0, 0.0).astype(BF16)
    needed = jnp.max(first).astype(jnp.int32)
    budget = jnp.int32(0)
    for rows in BUDGETS[:-1]:
        budget = budget + (needed > rows).astype(jnp.int32)
    budget_ref[0] = budget


def pack(incoming):
    blocks, block_rows, width = incoming.shape
    rows = blocks * CAP
    vmem = pl.BlockSpec(memory_space=pltpu.VMEM)
    return pl.pallas_call(
        packing_kernel,
        out_shape=(
            jax.ShapeDtypeStruct((rows, width), BF16),
            jax.ShapeDtypeStruct((rows, blocks * block_rows), BF16),
            jax.ShapeDtypeStruct((1,), jnp.int32),
        ),
        in_specs=[vmem],
        out_specs=(vmem, vmem, pl.BlockSpec(memory_space=pltpu.SMEM)),
        compiler_params=pltpu.CompilerParams(vmem_limit_bytes=6 * 2**20),
        cost_estimate=pl.CostEstimate(flops=2 * rows * rows * width, bytes_accessed=6 * rows * width, transcendentals=0),
        name="pack",
    )(incoming)


def expert_kernel(
    cols_hbm, router_ref, up_hbm, down_hbm, part_hbm, terms_ref, cols, up, down, part, acc, sems
):
    tiles, rows, width = cols.shape
    pair = tiles // STEPS
    deep = pair * width

    def load_cols(c):
        return pltpu.make_async_copy(
            cols_hbm.at[pl.ds(c * pair, pair)], cols.at[pl.ds(c * pair, pair)], sems.at[0, c]
        )

    def load_up(c):
        return pltpu.make_async_copy(up_hbm.at[0, pl.ds(c * deep, deep)], up.at[c], sems.at[1, c])

    def load_down(c):
        return pltpu.make_async_copy(
            down_hbm.at[0, :, pl.ds(c * deep, deep)], down.at[c], sems.at[2, c]
        )

    def store_part(c):
        return pltpu.make_async_copy(
            part.at[pl.ds(c * pair, pair)], part_hbm.at[pl.ds(c * pair, pair)], sems.at[3, c]
        )

    for c in range(STEPS):
        load_cols(c).start()
        load_up(c).start()
    for c in range(STEPS):
        load_down(c).start()
    squares = jnp.zeros((rows, 1), F32)
    logits = jnp.zeros((rows, 1), F32)
    acc[...] = jnp.zeros_like(acc)

    def up_step(c, sums):
        squares, logits = sums
        load_cols(c).wait()
        load_up(c).wait()
        pieces = [cols[c * pair + i] for i in range(pair)]
        acc[...] += jnp.dot(jnp.concatenate(pieces, axis=1), up[c], preferred_element_type=F32)
        for i in range(pair):
            piece = pieces[i].astype(F32)
            squares = squares + jnp.sum(piece * piece, axis=1, keepdims=True)
            logits = logits + jnp.sum(
                piece * router_ref[pl.ds(c * pair + i, 1)], axis=1, keepdims=True
            )
        return squares, logits

    squares, logits = lax.fori_loop(0, STEPS, up_step, (squares, logits))
    inv_rms = lax.rsqrt(squares / DM + 1e-06)
    up_sum = acc[...] * inv_rms
    hidden = (up_sum / (1.0 + jnp.exp(-up_sum))).astype(BF16)
    logit = logits * inv_rms
    high = logit.astype(BF16)
    rest = logit - high.astype(F32)
    middle = rest.astype(BF16)
    low = rest - middle.astype(F32)
    lane = lax.broadcasted_iota(jnp.int32, (rows, 128), 1)
    terms_ref[...] = jnp.where(
        lane == 0,
        high.astype(F32),
        jnp.where(lane == 1, middle.astype(F32), jnp.where(lane == 2, low, 0.0)),
    ).astype(BF16)

    def down_step(c, carry):
        load_down(c).wait()
        out = jnp.dot(hidden, down[c], preferred_element_type=F32).astype(BF16)
        for i in range(pair):
            part[c * pair + i] = out[:, i * width : (i + 1) * width]
        store_part(c).start()
        return carry

    lax.fori_loop(0, STEPS, down_step, 0)
    for c in range(STEPS):
        store_part(c).wait()


def expert(columns, own_router, up_weight, down_weight):
    tiles, rows, width = columns.shape
    hidden_units = up_weight.shape[2]
    deep = tiles // STEPS * width
    anywhere = pl.BlockSpec(memory_space=pl.ANY)
    far = pl.BlockSpec(memory_space=pltpu.HBM)
    vmem = pl.BlockSpec(memory_space=pltpu.VMEM)
    return pl.pallas_call(
        expert_kernel,
        out_shape=(
            jax.ShapeDtypeStruct((tiles, rows, width), BF16),
            jax.ShapeDtypeStruct((rows, 128), BF16),
        ),
        in_specs=[anywhere, vmem, far, far],
        out_specs=(anywhere, vmem),
        scratch_shapes=[
            pltpu.VMEM((tiles, rows, width), BF16),
            pltpu.VMEM((STEPS, deep, hidden_units), BF16),
            pltpu.VMEM((STEPS, hidden_units, deep), BF16),
            pltpu.VMEM((tiles, rows, width), BF16),
            pltpu.VMEM((rows, hidden_units), F32),
            pltpu.SemaphoreType.DMA((4, STEPS)),
        ],
        compiler_params=pltpu.CompilerParams(vmem_limit_bytes=40 * 2**20),
        cost_estimate=pl.CostEstimate(
            flops=4 * rows * tiles * width * hidden_units,
            bytes_accessed=4 * tiles * width * (hidden_units + rows),
            transcendentals=rows * hidden_units,
        ),
        name="expert",
    )(columns, own_router, up_weight, down_weight)


def local(
    mixer_input,
    gate_input,
    conv_state,
    conv_weight,
    conv_bias,
    state_proj,
    step_proj,
    step_bias,
    decay_rate,
    skip_gain,
    scan_state,
    output_proj,
    residual,
    router,
    expert_ids,
    active,
    up_weight,
    down_weight,
):
    n_tensor = lax.axis_size("tensor")
    experts_total = router.shape[1]
    sessions = expert_ids.shape[0]
    slice_width = residual.shape[1]
    low_rank = step_proj.shape[0]
    states = decay_rate.shape[0]

    live_float = active.astype(F32)
    live_mask = active == 1
    flat_ids = expert_ids.reshape(-1)
    flat_live = jnp.broadcast_to(live_mask[:, None], (sessions, 2)).reshape(-1)
    pairs = jnp.arange(flat_ids.shape[0], dtype=jnp.int32)
    earlier = (
        (flat_ids[:, None] == flat_ids[None, :])
        & (pairs[None, :] < pairs[:, None])
        & flat_live[None, :]
    )
    slot_index = jnp.sum(earlier.astype(jnp.int32), axis=1).reshape(sessions, 2)
    buffer_row = jnp.where(live_mask[:, None], expert_ids * CAP + slot_index, -1)
    row_numbers = jnp.arange(experts_total * CAP, dtype=jnp.int32)
    out_numbers = jnp.arange(experts_total * STRIDE, dtype=jnp.int32)
    out_row = jnp.where(live_mask[:, None], expert_ids * STRIDE + slot_index, -1)
    placement = jnp.any(out_row[None] == out_numbers[:, None, None], axis=2)
    counting = (out_numbers[:, None] // STRIDE == jnp.arange(experts_total, dtype=jnp.int32)[None]) & (
        out_numbers[:, None] % STRIDE >= CAP
    )
    placement = jnp.concatenate([placement, counting], axis=1).astype(BF16)
    live_counts = jnp.sum(
        (flat_ids[None] == jnp.arange(experts_total, dtype=jnp.int32)[:, None]) & flat_live[None],
        axis=1,
    ).astype(BF16)

    window = jnp.concatenate([conv_state, mixer_input[:, None, :]], axis=1)
    conv_sum = jnp.sum(window.astype(F32) * conv_weight[None], axis=1) + conv_bias
    conv_out = jax.nn.silu(conv_sum).astype(BF16)
    partial_proj = jnp.dot(conv_out, state_proj, preferred_element_type=F32).astype(BF16)
    projected = sum_everywhere(partial_proj)
    step_raw = projected[:, :low_rank]
    input_map = projected[:, low_rank : low_rank + states]
    output_map = projected[:, low_rank + states :]
    step_norm = (
        step_raw * lax.rsqrt(jnp.mean(step_raw * step_raw, axis=1, keepdims=True) + 1e-06)
    ).astype(BF16)
    step_size = jax.nn.softplus(jnp.dot(step_norm, step_proj, preferred_element_type=F32) + step_bias)
    conv_float = conv_out.astype(F32)
    state_next = (
        jnp.exp(-step_size[:, None, :] * decay_rate[None]) * scan_state
        + (step_size * conv_float)[:, None, :] * input_map[:, :, None]
    )
    scan_out = jnp.sum(output_map[:, :, None] * state_next, axis=1) + skip_gain * conv_float
    gated = (scan_out * jax.nn.silu(gate_input.astype(F32)) * live_float[:, None]).astype(BF16)
    state_out = jnp.where(live_mask[:, None, None], state_next, scan_state)
    conv_cache = jnp.where(live_mask[:, None, None], window[:, 1:, :], conv_state)
    mixer_part = jnp.dot(gated, output_proj, preferred_element_type=F32).astype(BF16)
    hidden_local = sum_over_tensor(
        mixer_part.reshape(sessions, n_tensor, slice_width).transpose(1, 0, 2)
    ) + residual.astype(F32)

    sources = jnp.concatenate(
        [
            hidden_local.astype(BF16),
            jnp.broadcast_to(live_counts[:, None], (experts_total, slice_width)),
        ],
        axis=0,
    )
    outgoing = jnp.dot(placement, sources, preferred_element_type=F32).astype(BF16)
    outgoing = outgoing.reshape(experts_total, STRIDE, slice_width)
    incoming = lax.all_to_all(outgoing, "dp", split_axis=0, concat_axis=0, tiled=True)
    packed, spread, budget = pack(incoming)
    own_router = lax.dynamic_slice_in_dim(router, lax.axis_index("dp"), 1, 1)[:, 0]
    own_router = own_router.astype(F32).reshape(n_tensor, slice_width)

    def on_rows(rows):
        def run(packed, spread, own_router, up_weight, down_weight):
            columns = lax.all_to_all(
                jnp.broadcast_to(packed[None, :rows], (n_tensor, rows, slice_width)),
                "tensor",
                split_axis=0,
                concat_axis=0,
                tiled=True,
            )
            expert_part, terms = expert(columns, own_router, up_weight, down_weight)
            share = jnp.concatenate([sum_over_tensor(expert_part).astype(BF16), terms], axis=1)
            return jnp.dot(spread[:, :rows], share, preferred_element_type=F32).astype(BF16)

        return run

    replies = lax.switch(
        budget[0], [on_rows(rows) for rows in BUDGETS], packed, spread, own_router, up_weight, down_weight
    )

    returned = lax.all_to_all(
        replies.reshape(experts_total, CAP, slice_width + 128),
        "dp",
        split_axis=0,
        concat_axis=0,
        tiled=True,
    ).reshape(experts_total * CAP, slice_width + 128)
    chosen = buffer_row.reshape(-1)[:, None] == row_numbers[None]
    gathered = jnp.dot(chosen.astype(BF16), returned, preferred_element_type=F32).reshape(
        sessions, 2, slice_width + 128
    )
    chosen_logit = gathered[:, :, slice_width] + (
        gathered[:, :, slice_width + 1] + gathered[:, :, slice_width + 2]
    )
    first = 1.0 / (1.0 + jnp.exp(chosen_logit[:, 1] - chosen_logit[:, 0]))
    second = 1.0 / (1.0 + jnp.exp(chosen_logit[:, 0] - chosen_logit[:, 1]))
    route_weight = jnp.stack([first, second], axis=1) * live_float[:, None]
    layer_out = (hidden_local + jnp.sum(route_weight[:, :, None] * gathered[:, :, :slice_width], axis=1)).astype(BF16)
    return (layer_out, state_out, conv_cache)


def solution(mesh):
    placed = (
        P("dp", "tensor"),
        P("dp", "tensor"),
        P("dp", None, "tensor"),
        P(None, "tensor"),
        P("tensor"),
        P("tensor", None),
        P(None, "tensor"),
        P("tensor"),
        P(None, "tensor"),
        P("tensor"),
        P("dp", None, "tensor"),
        P("tensor", None),
        P("dp", "tensor"),
        P(),
        P("dp", None),
        P("dp"),
        P("dp", None, "tensor"),
        P("dp", "tensor", None),
    )
    return jax.shard_map(
        local,
        mesh=mesh,
        in_specs=placed,
        out_specs=(P("dp", "tensor"), P("dp", None, "tensor"), P("dp", None, "tensor")),
        check_vma=False,
    )
```
